256 devices in a mesh: gx: 16 (over z, core), gy: 4 (over x), gz: 4 (over y).
Axes of the slice: x: 4, y: 4, z: 8, core: 2. Of those that a mesh axis runs over, the one named last changes fastest.
Arguments:
- displacement: float32 [3, 64, 32, 2048], P(None, 'gz', 'gy', 'gx'), may hold values from -4 to 4
- direction: float32 [3, 64, 32, 2048], P(None, 'gz', 'gy', 'gx'), may hold values from -6 to 6
- modulus: float32 [64, 32, 2048], P('gz', 'gy', 'gx'), may hold values from 0.5 to 5
- external: float32 [3, 64, 32, 2048], P(None, 'gz', 'gy', 'gx'), may hold values from -6 to 6
- stiffness: float32 [81, 81], replicated, as said below
- master_record: float32 [27, 524288], P(None, ('gx', 'gy', 'gz')), may hold values from -1 to 1
- pair_face: int32 [262144], P(('gx', 'gy', 'gz')), may hold values from 0 to 188
- pair_owner: int32 [262144, 1], P(('gx', 'gy', 'gz')), may hold values from 0 to 63; in each aligned block of 1024 rows (0 to 1023, 1024 to 2047, ...) at most 32 rows name the same one
- pair_row: int32 [262144], P(('gx', 'gy', 'gz')), may hold values from 0 to 2047
- pair_count: int32 [256], P(('gx', 'gy', 'gz')), may hold values from 1 to 1024, 104857 in all
Outputs:
- residual: float32 [3, 64, 32, 2048], P(None, 'gz', 'gy', 'gx')
- tangent: float32 [3, 64, 32, 2048], P(None, 'gz', 'gy', 'gx')
The draws below stay inside these ranges and needn't reach their ends.
Inputs may be any that keep to these rules, and one draw needn't show every extreme that they name: `pair_owner`: among the pair slots of one device, at most 32 name the same owner, a bound that the slots of some device reach. `pair_count`: the busiest device has all 1024 slots live; the counts sum to 104857. `stiffness`: symmetric with a dominant positive diagonal.
All inputs are finite; a program needn't handle non-finite values.
Results may differ from the reference program's by a relative error of at most 0.00011.
Values sent between devices are 32-bit elements; how exact they have to be, the bound alone decides.
No kernel may reach another device: no remote copies, remote signals or barrier semaphores. Data moves between devices by JAX's collectives and lax.ppermute only.
A program may use at most 128 MiB of HBM per device.

```python
import math
import jax
import jax.numpy as jnp
import numpy as np
from jax import lax

EX = 64
EY = 4
EZ = 8
PAIR_DEV = 1024
MSEG_DEV = 2048
CAP = 32
NX = 2048
NY = 32
NZ = 64
MSEG = 524288
N_GX = 16
N_GY = 4
N_GZ = 4
DEVICES = 256


def draw_stiffness(key, part):
    raw = jax.random.normal(key, (81, 81), jnp.float32) * 0.1
    symmetric = (raw + raw.T) * 0.5
    diagonal = jax.random.uniform(jax.random.fold_in(key, 1), (81,), jnp.float32, minval=1.5, maxval=3.0)
    return (0.25 * (symmetric + jnp.diag(diagonal))).astype(jnp.float32)


def touch_ends(values, stream_key, low, top_value):
    spot = [jax.random.randint(jax.random.fold_in(stream_key, axis), (), 0, length) for axis, length in enumerate(values.shape)]
    longest = values.shape.index(max(values.shape))
    beside = spot[:longest] + [(spot[longest] + 1) % values.shape[longest]] + spot[longest + 1:]
    return values.at[tuple(spot)].set(low).at[tuple(beside)].set(top_value)


def levels(rng, shape, cuts, low, largest):
    factor_of = 1.0
    for dim, parts in cuts:
        steps = jax.random.uniform(jax.random.fold_in(jax.random.fold_in(rng, 6), dim), (parts,), jnp.float32, low / len(cuts), largest / len(cuts))
        factor_of = factor_of * jnp.repeat(jnp.exp(steps), shape[dim] // parts).reshape((-1,) + (1,) * (len(shape) - 1 - dim))
    return factor_of


def profile(count, total, reach, skew):
    weights = [(1 << 20) // math.isqrt(rank ** skew) + 1 for rank in range(2, count + 1)]
    surplus, holding = total - reach - (count - 1), [1] * (count - 1)
    while surplus > 0:
        movable = [i for i in range(count - 1) if holding[i] < reach]
        mass, budget = sum([weights[i] for i in movable]), surplus
        for i in movable:
            extra = min(reach - holding[i], max(1, budget * weights[i] // mass), surplus)
            holding[i] = holding[i] + extra
            surplus = surplus - extra
    return np.array([reach] + holding)


def ragged_sizes(rng, amount, total, limit, skew):
    if amount == 2:
        one = jax.random.randint(rng, (), max(1, total - limit), min(limit, total - 1) + 1)
        return jnp.stack([one, total - one])
    tallies = jnp.asarray(profile(amount, total, limit, skew), jnp.int32)
    pairs = (amount - 1) // 2
    source_of, sink = tallies[1:1 + 2 * pairs:2], tallies[2:2 + 2 * pairs:2]
    slack = jnp.minimum(source_of - 1, limit - sink)
    moved = jax.random.randint(jax.random.fold_in(rng, 1), (pairs,), 0, 1 << 20) % (slack + 1)
    tallies = tallies.at[1:1 + 2 * pairs:2].set(source_of - moved).at[2:2 + 2 * pairs:2].set(sink + moved)
    return tallies[jax.random.permutation(jax.random.fold_in(rng, 2), amount)]


def deal_out(rng, own, number, rows, count, top, reach, skew):
    sequence = jax.random.permutation(rng, count)
    heavy_load, usual = load_shares(count, rows * top, reach, skew, True), load_shares(count, rows * top, reach, skew, False)
    places = jnp.arange(count)

    def named(lengths, offset_by):
        used = int((lengths > 0).sum())
        fixed = max(1, used // 4)
        moved = fixed + (places - fixed + offset_by * (used - fixed)) % max(1, count - fixed)
        return jnp.zeros((count,), jnp.int32).at[sequence[jnp.where(places < fixed, places, moved)]].set(jnp.asarray(lengths, jnp.int32))

    lengths = jnp.where(number % 4 == 0, named(heavy_load, number // 4), named(usual, number - number // 4 - 1))
    mixed = jax.random.permutation(jax.random.fold_in(own, 3), count)
    donor, taker = mixed[0:count // 2 * 2:2], mixed[1:count // 2 * 2:2]
    slack = jnp.minimum(lengths[donor] - 1, reach - lengths[taker]) // 2
    slack = jnp.where((donor == sequence[0]) | (taker == sequence[0]) | (lengths[taker] == 0), 0, jnp.maximum(slack, 0))
    moved = jax.random.randint(jax.random.fold_in(own, 4), (count // 2,), 0, 1 << 20) % (slack + 1)
    lengths = lengths.at[donor].add(-moved).at[taker].add(moved)
    members = jnp.searchsorted(jnp.cumsum(lengths), jnp.arange(rows * top), side="right").astype(jnp.int32)
    listing = members.reshape(top, rows).T
    listing = listing[jax.random.permutation(jax.random.fold_in(own, 1), rows)]
    offset_by = jax.random.randint(jax.random.fold_in(own, 2), (rows, 1), 0, top)
    return jnp.take_along_axis(listing, (jnp.arange(top)[None, :] + offset_by) % top, axis=1)


def load_shares(count, total, limit, skew, full):
    loads = [(1 << 20) // math.isqrt(standing ** skew) + 1 for standing in range(1, count + 1)]
    largest = limit if full else min(limit, max(-(-total // count), total * loads[0] // sum(loads)))
    least = 1 if total - largest >= count - 1 else 0
    holding, spare = [largest] + [least] * (count - 1), total - largest - least * (count - 1)
    while spare > 0:
        movable = [i for i in range(1, count) if holding[i] < largest] or [i for i in range(1, count) if holding[i] < limit]
        mass, left = sum([loads[i] for i in movable]), spare
        for i in movable:
            addition = min(limit - holding[i], max(1, left * loads[i] // mass), spare)
            holding[i] = holding[i] + addition
            spare = spare - addition
    return np.array(holding)


def centred(rng, extent, deviation, reach, split=(), kind=jnp.bfloat16):
    values = jax.random.normal(rng, extent, jnp.float32) * deviation
    if len(split) > 0:
        values = levels(rng, extent, split, -0.22, 0.18) * values
    return jnp.clip(values, min=-reach, max=reach).astype(kind)


def setup_inputs(seed: int = 0) -> dict:
    splits = jax.random.split(jax.random.key(seed), 11)
    displacement = centred(splits[0], (3, NZ, NY, NX), 0.5, 4.0, ((1, 4), (2, 4), (3, 16)), jnp.float32)
    direction = centred(splits[1], (3, NZ, NY, NX), 1.0, 6.0, ((1, 4), (2, 4), (3, 16)), jnp.float32)
    modulus = jnp.clip(jnp.exp(math.log(5.0) - 2.3025851 * jax.random.uniform(splits[2], (NZ, NY, NX), jnp.float32) ** levels(splits[2], (NZ, NY, NX), ((0, 4), (1, 4), (2, 16)), -0.2, 0.2)), 0.5, 5.0)
    external = centred(splits[3], (3, NZ, NY, NX), 1.0, 6.0, ((1, 4), (2, 4), (3, 16)), jnp.float32)
    stiffness = draw_stiffness(jax.random.fold_in(splits[10], 71), 0)
    master_record = jnp.clip(jax.random.uniform(splits[5], (27, MSEG), jnp.float32, -1.0, 1.0) * levels(splits[5], (27, MSEG), ((1, 256),), -0.4, 0.0), -1.0, 1.0)
    pair_face = touch_ends(jax.random.randint(splits[6], (DEVICES * PAIR_DEV,), 0, (EX - 1) * (EY - 1)), jax.random.fold_in(splits[6], 1), 0, ((EX - 1) * (EY - 1)) - 1).astype(jnp.int32)
    pair_owner_keys = jax.random.split(jax.random.fold_in(splits[7], 1), (DEVICES * PAIR_DEV) // PAIR_DEV)
    pair_owner_turns = jax.random.permutation(jax.random.fold_in(splits[7], 3), (DEVICES * PAIR_DEV) // PAIR_DEV)
    pair_owner = jax.vmap(lambda own, number: deal_out(jax.random.fold_in(splits[7], 2), own, number, PAIR_DEV, N_GX * N_GY, 1, CAP, 2))(pair_owner_keys, pair_owner_turns).reshape((DEVICES * PAIR_DEV, 1))
    pair_row = touch_ends(jax.random.randint(splits[8], (DEVICES * PAIR_DEV,), 0, MSEG_DEV), jax.random.fold_in(splits[8], 1), 0, MSEG_DEV - 1).astype(jnp.int32)
    pair_count = ragged_sizes(splits[9], DEVICES, DEVICES * PAIR_DEV * 2 // 5, PAIR_DEV, 2).astype(jnp.int32)
    return {"displacement": displacement, "direction": direction, "modulus": modulus, "external": external, "stiffness": stiffness, "master_record": master_record, "pair_face": pair_face, "pair_owner": pair_owner, "pair_row": pair_row, "pair_count": pair_count}


BETA_CUBIC = 0.1
PENALTY = 4.0
SMOOTHING = 0.5
HIGHEST = lax.Precision.HIGHEST

def face_tables():
    points = np.array([-np.sqrt(0.6), 0.0, np.sqrt(0.6)])
    gauss_w = np.array([5.0, 8.0, 5.0]) / 9.0
    line_shape = np.stack([points * (points - 1.0) / 2.0, 1.0 - points * points, points * (points + 1.0) / 2.0], axis=1)
    table = (line_shape[:, None, :, None] * line_shape[None, :, None, :]).reshape(9, 9)
    weights = np.outer(gauss_w, gauss_w).reshape(9) * 0.25
    return (jnp.asarray(table, jnp.float32), jnp.asarray(table * weights[:, None], jnp.float32))

def integrate(slave_u, slave_v, record):
    table, weighted = face_tables()
    slots = slave_u.shape[-1]
    u_points = jnp.einsum('qa,acs->qcs', table, slave_u.reshape(9, 3, slots), precision=HIGHEST)
    v_points = jnp.einsum('qa,acs->qcs', table, slave_v.reshape(9, 3, slots), precision=HIGHEST)
    m_points = jnp.einsum('qa,kas->kqs', table, record.reshape(3, 9, slots), precision=HIGHEST)
    gap_value = m_points[0] + m_points[1] * u_points[:, 0] + m_points[2] * u_points[:, 1] + u_points[:, 2]
    scaled = -gap_value / SMOOTHING
    pressure = PENALTY * SMOOTHING * jax.nn.softplus(scaled)
    slope = PENALTY * jax.nn.sigmoid(scaled)
    normal_dot = m_points[1] * v_points[:, 0] + m_points[2] * v_points[:, 1] + v_points[:, 2]
    normal = jnp.stack([m_points[1], m_points[2], jnp.ones_like(m_points[1])], axis=1)
    res_part = -jnp.einsum('qa,qcs->acs', weighted, pressure[:, None] * normal, precision=HIGHEST)
    tan_part = jnp.einsum('qa,qcs->acs', weighted, (slope * normal_dot)[:, None] * normal, precision=HIGHEST)
    return (res_part.reshape(27, slots), tan_part.reshape(27, slots))

def element_block(nodes, stiffness, valid):
    za = (nodes.shape[1] - 1) // 2
    yb = (nodes.shape[2] - 1) // 2
    xc = (nodes.shape[3] - 1) // 2
    elems = za * yb * xc
    pieces = []
    for r in range(3):
        for q in range(3):
            for p in range(3):
                pieces.append(nodes[:, r:r + 2 * za:2, q:q + 2 * yb:2, p:p + 2 * xc:2].reshape(7, elems))
    gathered = jnp.stack(pieces, axis=0)
    disp_dofs = gathered[:, 0:3].reshape(81, elems)
    dir_dofs = gathered[:, 3:6].reshape(81, elems)
    coeff = lax.optimization_barrier(jnp.mean(gathered[:, 6], axis=0)) * valid
    both = jnp.dot(stiffness, jnp.concatenate([disp_dofs, dir_dofs], axis=1), precision=HIGHEST)
    force = coeff * (both[:, :elems] + BETA_CUBIC * disp_dofs ** 3)
    image = coeff * (both[:, elems:] + 3.0 * BETA_CUBIC * disp_dofs * disp_dofs * dir_dofs)
    result = jnp.concatenate([force.reshape(27, 3, elems), image.reshape(27, 3, elems)], axis=1).reshape(27, 6, za, yb, xc)
    total = jnp.zeros((6,) + nodes.shape[1:], jnp.float32)
    for r in range(3):
        for q in range(3):
            for p in range(3):
                total = total.at[:, r:r + 2 * za:2, q:q + 2 * yb:2, p:p + 2 * xc:2].add(result[9 * r + 3 * q + p])
    return total

def reference(displacement, direction, modulus, external, stiffness, master_record, pair_face, pair_owner, pair_row, pair_count):
    stacked = jnp.concatenate([displacement, direction, modulus[None]], axis=0)

    def layer(index, total):
        start = (2 * index).astype(jnp.int32)
        zero = jnp.int32(0)
        block = lax.dynamic_slice(stacked, (zero, start, zero, zero), (7, 3, NY - 1, NX - 1))
        part = element_block(block, stiffness, 1.0)
        old = lax.dynamic_slice(total, (zero, start, zero, zero), (6, 3, NY - 1, NX - 1))
        return lax.dynamic_update_slice(total, old + part, (zero, start, zero, zero))
    total = lax.fori_loop(0, NZ // 2 - 1, layer, jnp.zeros((6, NZ, NY, NX), jnp.float32))
    all_pairs = N_GX * N_GY * N_GZ * PAIR_DEV
    slot_ids = jnp.arange(all_pairs, dtype=jnp.int32)
    device = slot_ids // PAIR_DEV
    gx_index = device // (N_GY * N_GZ)
    gy_index = device // N_GZ % N_GY
    gz_index = device % N_GZ
    live = slot_ids % PAIR_DEV < pair_count[device]
    face_row = pair_face // (EX - 1)
    face_col = pair_face % (EX - 1)
    local_node = jnp.arange(9, dtype=jnp.int32)
    y_node = gy_index[None, :] * (2 * EY) + 2 * face_row[None, :] + (local_node // 3)[:, None]
    x_node = gx_index[None, :] * (2 * EX) + 2 * face_col[None, :] + (local_node % 3)[:, None]
    z_node = gz_index[None, :] * (2 * EZ)
    node_index = ((z_node * NY + y_node) * NX + x_node).astype(jnp.int32)
    column = ((pair_owner[:, 0] * N_GZ + gz_index) * MSEG_DEV + pair_row).astype(jnp.int32)
    surface_u = jnp.take(displacement.reshape(3, -1), node_index, axis=1).transpose(1, 0, 2).reshape(27, all_pairs)
    surface_v = jnp.take(direction.reshape(3, -1), node_index, axis=1).transpose(1, 0, 2).reshape(27, all_pairs)
    record = jnp.take(master_record, column, axis=1)
    res_part, tan_part = integrate(surface_u, surface_v, record)
    contact = jnp.where(live[None, :], jnp.concatenate([res_part, tan_part], axis=0), 0.0)
    spread = contact.reshape(2, 9, 3, all_pairs).transpose(0, 2, 1, 3).reshape(6, 9, all_pairs)
    surface = jnp.zeros((6, NZ * NY * NX), jnp.float32).at[:, node_index].add(spread).reshape(6, NZ, NY, NX)
    total = total + surface
    return (total[:3] - external, total[3:])
```

```python
import jax
import jax.numpy as jnp
import numpy as np
from jax import lax
from jax.experimental import pallas as pl
from jax.experimental.pallas import tpu as pltpu
from jax.sharding import PartitionSpec as P

F32 = jnp.float32
BF16 = jnp.bfloat16
I32 = jnp.int32

ZN, YN, XN = 16, 8, 128
ZE, YE = ZN + 3, YN + 3
OWNERS, CAP, PAIRS, ROWS = 64, 32, 1024, 2048
CHUNKS = OWNERS * CAP // 128
FACE_ROWS, FACE_COLS, FACE_LANES = 3, 63, 64
FACES = FACE_ROWS * FACE_LANES
SLABS = 28
TILE = 16
YPITCH = TILE
ZPITCH = YE * TILE
NODE_ROWS = ZE * ZPITCH
BLOCK = 9 * TILE
GROUPS = ("gx", "gy")


def shapes_1d():
    points = np.array([-np.sqrt(0.6), 0.0, np.sqrt(0.6)])
    gauss = np.array([5.0, 8.0, 5.0]) / 9.0
    line = np.stack(
        [points * (points - 1.0) / 2.0, 1.0 - points * points, points * (points + 1.0) / 2.0],
        axis=1,
    )
    return line, gauss


def halves(values):
    high = np.asarray(values, np.float32).astype(jnp.bfloat16)
    low = (np.asarray(values, np.float64) - high.astype(np.float64)).astype(jnp.bfloat16)
    return high, low


def record_map():
    line, _ = shapes_1d()
    out = np.zeros((32, 27))
    for k in range(3):
        for qy in range(3):
            for qx in range(3):
                q = 3 * qy + qx
                row = k * 8 + q if q < 8 else 24 + k
                for b in range(3):
                    for a in range(3):
                        out[row, 9 * k + 3 * b + a] = line[qy, b] * line[qx, a]
    return halves(out)


def quad_row(part, q):
    return part * 8 + q if q < 8 else 48 + part


def face_x_map():
    line, _ = shapes_1d()
    out = np.zeros((128, 6 * 128))
    for qx in range(3):
        for side in range(2):
            for fx in range(FACE_COLS):
                for a in range(3):
                    out[2 * fx + a, (2 * qx + side) * 128 + side * 64 + fx] = line[qx, a]
    return halves(out)


def face_y_map():
    line, _ = shapes_1d()
    first = np.zeros((56, 6 * 48))
    second = np.zeros((56, 6 * 48))
    for part in range(6):
        for qy in range(3):
            for qx in range(3):
                row = quad_row(part, 3 * qy + qx)
                for b in range(3):
                    first[row, (2 * qx) * 48 + part * 8 + b] = line[qy, b]
                    first[row, (2 * qx + 1) * 48 + part * 8 + 2 + b] = line[qy, b]
                    second[row, (2 * qx) * 48 + part * 8 + 4 + b] = line[qy, b]
    return halves(first), halves(second)


def node_x_map():
    line, _ = shapes_1d()
    out = np.zeros((FACE_LANES, 3 * 128))
    for qx in range(3):
        for fx in range(FACE_COLS):
            for a in range(3):
                out[fx, qx * 128 + 2 * fx + a] = line[qx, a]
    return halves(out)


def node_y_map():
    line, gauss = shapes_1d()
    out = np.zeros((48, 3 * FACE_ROWS * 64))
    for part in range(6):
        for qx in range(3):
            for qy in range(3):
                weight = 0.25 * gauss[qx] * gauss[qy] * (-1.0 if part < 3 else 1.0)
                for fy in range(FACE_ROWS):
                    for b in range(3):
                        column = qx * FACE_ROWS * 64 + fy * 64 + quad_row(part, 3 * qy + qx)
                        out[part * 8 + 2 * fy + b, column] = weight * line[qy, b]
    return halves(out)


def stiffness_places():
    place = np.zeros((BLOCK, 81))
    for block in range(9):
        for p in range(3):
            for c in range(3):
                place[block * TILE + 3 * p + c, block * 9 + 3 * p + c] = 1.0
    fixed = np.zeros((BLOCK, BLOCK))
    for block in range(9):
        fixed[block * TILE + 9, block * TILE + 12] = 1.0
        for p in range(3):
            fixed[10, block * TILE + 9 + p] = 1.0 / 27.0
    fixed[[b * TILE + 9 for b in range(1, 9)], :] = 0.0
    for block in range(1, 9):
        fixed[block * TILE + 9, block * TILE + 12] = 1.0
    return place.astype(np.float32), halves(fixed)


def split(values):
    high = values.astype(BF16)
    return high, (values - high.astype(F32)).astype(BF16)


def mm(a, b):
    return jnp.dot(a, b, preferred_element_type=F32)


def mm_nt(a, b):
    return lax.dot_general(a, b, (((1,), (1,)), ((), ())), preferred_element_type=F32)


def mm3(a, b):
    return mm(a[0], b[0]) + (mm(a[0], b[1]) + mm(a[1], b[0]))


def lane_ids(rows):
    return lax.broadcasted_iota(I32, (rows, 128), 1)


def pick_lanes(values, index):
    return jnp.take_along_axis(values, index, axis=1, mode="promise_in_bounds")


def compact(values):
    return (
        values[0:16]
        + pltpu.roll(values[16:32], 32, 1)
        + pltpu.roll(values[32:48], 64, 1)
        + pltpu.roll(values[48:64], 96, 1)
    )


def swap_groups(parts):
    group = lane_ids(8) // 32
    out = []
    for f in range(4):
        total = None
        for g in range(4):
            moved = parts[g] if f == g else pltpu.roll(parts[g], (32 * (g - f)) % 128, 1)
            total = moved if total is None else jnp.where(group == g, moved, total)
        out.append(total)
    return out


def request_kernel(owner, row, face, count, u, v, m, request, faces, z_up, z_down):
    for first, field, comps in ((0, u, 3), (3, v, 3), (6, m, 1)):
        for c in range(comps):
            z_up[first + c] = field[pl.ds((c * ZN + ZN - 2) * YN, 2 * YN), :]
            z_down[first + c] = field[pl.ds(c * ZN * YN, YN), :]
    live_count = count[0]
    who = lax.broadcasted_iota(I32, (OWNERS, 128), 0)
    lane = lane_ids(1)
    hits = []
    for t in range(PAIRS // 128):
        live = lane + t * 128 < live_count
        target = jnp.where(live, owner[pl.ds(t, 1), :], -1)
        hits.append(jnp.where(who == target, 1.0, 0.0).astype(F32))
    before = jnp.where(
        lax.broadcasted_iota(I32, (128, 128), 0) < lax.broadcasted_iota(I32, (128, 128), 1), 1.0, 0.0
    ).astype(BF16)
    ranks = mm(jnp.concatenate([h.astype(BF16) for h in hits], axis=0), before)
    base = jnp.zeros((OWNERS, 1), F32)
    places = lax.broadcasted_iota(I32, (128, 128), 0)
    highs, lows, sides = [], [], []
    for t in range(PAIRS // 128):
        rank = jnp.sum(hits[t] * (ranks[t * OWNERS : (t + 1) * OWNERS] + base), axis=0, keepdims=True)
        base = base + jnp.sum(hits[t], axis=1, keepdims=True)
        here = places == rank.astype(I32)
        number = row[pl.ds(t, 1), :] + 1
        f = face[pl.ds(t, 1), :]
        f = f + jnp.where(f >= FACE_COLS, 1, 0) + jnp.where(f >= 2 * FACE_COLS, 1, 0) + 1
        highs.append(jnp.where(here, lax.shift_right_logical(number, 6).astype(F32), 0.0).astype(BF16))
        lows.append(jnp.where(here, (number & 63).astype(F32), 0.0).astype(BF16))
        sides.append(jnp.where(here, f.astype(F32), 0.0).astype(BF16))
    hit = jnp.concatenate([h.astype(BF16) for h in hits], axis=1)
    high = mm_nt(hit, jnp.concatenate(highs, axis=1))
    low = mm_nt(hit, jnp.concatenate(lows, axis=1))
    request[...] = (high * 64.0 + low).astype(I32)
    faces[...] = compact(mm_nt(hit, jnp.concatenate(sides, axis=1))).astype(I32)


def prepare_kernel(
    u, v, m, z_low, z_high, stiffness, master, place, fixed_h, fixed_l, record_h, record_l,
    face_x_h, face_x_l, first_h, first_l, second_h, second_l,
    y_up, y_down, big_h, big_l, table, quads,
):
    for first, field, comps in ((0, u, 3), (3, v, 3), (6, m, 1)):
        for c in range(comps):
            n = first + c
            for out, h, y in ((y_up, 0, YN - 2), (y_up, 1, YN - 1), (y_down, 0, 0)):
                at = (n * (2 if out is y_up else 1) + h) * 24
                out[pl.ds(at, ZN), :] = field[pl.ds(c * ZN * YN + y, ZN, stride=YN), :]
                out[pl.ds(at + 16, 8), :] = jnp.zeros((8, 128), F32)
                out[pl.ds(at + 16, 1), :] = z_low[pl.ds((n * 2) * YN + y, 1), :]
                out[pl.ds(at + 17, 1), :] = z_low[pl.ds((n * 2 + 1) * YN + y, 1), :]
                out[pl.ds(at + 18, 1), :] = z_high[pl.ds(n * YN + y, 1), :]
    places = place[...]
    spread = jnp.dot(places, stiffness[...], precision=lax.Precision.HIGHEST, preferred_element_type=F32)
    spread = lax.dot_general(
        spread, places, (((1,), (1,)), ((), ())), precision=lax.Precision.HIGHEST, preferred_element_type=F32
    )
    high, low = split(spread)
    big_h[...] = high + fixed_h[...]
    big_l[...] = low + fixed_l[...]
    table[...] = mm3((record_h[...], record_l[...]), split(master[...]))
    plane = jnp.concatenate(
        [field[pl.ds(c * ZN * YN, YN), :] for field in (u, v) for c in range(3)], axis=0
    )
    wide = mm3(split(plane), (face_x_h[...], face_x_l[...]))
    tall = split(jnp.concatenate([wide[:, i * 128 : (i + 1) * 128] for i in range(6)], axis=0))
    quads[:, 0:128] = mm3((first_h[...], first_l[...]), tall)
    quads[:, 128:256] = mm3((second_h[...], second_l[...]), tall)


def gather_kernel(ids, table, reply):
    numbers = jnp.maximum(compact(ids[...]) - 1, 0)
    for c in range(CHUNKS):
        number = jnp.broadcast_to(numbers[c : c + 1], (8, 128))
        inside = number & 127
        outside = lax.shift_right_logical(number, 7)
        found = []
        for f in range(4):
            total = pick_lanes(table[pl.ds(f * 8, 8), 0:128], inside)
            for k in range(1, ROWS // 128):
                piece = pick_lanes(table[pl.ds(f * 8, 8), k * 128 : (k + 1) * 128], inside)
                total = jnp.where(outside == k, piece, total)
            found.append(total)
        for g, tile in enumerate(swap_groups(found)):
            reply[g * CHUNKS + c] = tile


def slabs_of(u, v, m, z_low, z_high, y_low, y_high):
    for first, field, comps in ((0, u, 3), (3, v, 3), (6, m, 1)):
        for c in range(comps):
            n = first + c
            for s in range(SLABS):
                if s < 16:
                    tile = field[pl.ds((c * ZN + s) * YN, YN), :]
                elif s < 18:
                    tile = z_low[pl.ds((n * 2 + s - 16) * YN, YN), :]
                elif s < 19:
                    tile = z_high[pl.ds(n * YN, YN), :]
                else:
                    h, zb = divmod(s - 19, 3)
                    if h < 2:
                        tile = y_low[pl.ds((n * 2 + h) * 24 + zb * 8, 8), :]
                    else:
                        tile = y_high[pl.ds(n * 24 + zb * 8, 8), :]
                yield n, s, tile


def edge_kernel(u, v, m, z_low, z_high, y_low, y_high, x_up, x_down):
    lane = lane_ids(8)
    up = [jnp.zeros((8, 128), F32) for _ in range(4)]
    down = [jnp.zeros((8, 128), F32) for _ in range(2)]
    for n, s, tile in slabs_of(u, v, m, z_low, z_high, y_low, y_high):
        i = n * SLABS + s
        k, spot = i // 64, i % 64
        moved = pltpu.roll(tile, (2 * spot - 126) % 128, 1)
        up[k] = jnp.where(lax.shift_right_logical(lane, 1) == spot, moved, up[k])
        k, spot = i // 128, i % 128
        moved = tile if spot == 0 else pltpu.roll(tile, spot, 1)
        down[k] = jnp.where(lane == spot, moved, down[k])
    for k in range(4):
        x_up[pl.ds(k * 8, 8), :] = up[k]
    for k in range(2):
        x_down[pl.ds(k * 8, 8), :] = down[k]


def element_kernel(
    edges, u, v, m, external, z_low, z_high, y_low, y_high, x_low, x_high, big_h, big_l,
    residual, tangent, nodes_u, nodes_v, tiles_h, tiles_l, total_u, total_v,
):
    lane = lane_ids(8)
    even = jnp.maximum(2 * (lane - 1), 0) & 127
    odd = jnp.maximum(2 * (lane - 1) + 1, 0) & 127
    after = (2 * lane) & 127
    for n, s, tile in slabs_of(u, v, m, z_low, z_high, y_low, y_high):
        i = n * SLABS + s
        k, spot = i // 64, i % 64
        left = x_low[pl.ds(k * 8, 8), :]
        k2, spot2 = i // 128, i % 128
        right = x_high[pl.ds(k2 * 8, 8), :]
        first = left if spot == 0 else pltpu.roll(left, (-2 * spot) % 128, 1)
        second = pltpu.roll(left, (-2 * spot - 1) % 128, 1)
        third = right if spot2 == 64 else pltpu.roll(right, (64 - spot2) % 128, 1)
        values = (
            jnp.where(lane == 0, first, pick_lanes(tile, even)),
            jnp.where(lane == 0, second, pick_lanes(tile, odd)),
            jnp.where(lane == 64, third, pick_lanes(tile, after)),
        )
        to = nodes_v if 3 <= n < 6 else nodes_u
        for p, value in enumerate(values):
            at = 9 + p if n == 6 else 3 * p + n % 3
            if s < 19:
                z = s + 2 if s < 16 else (0, 1, 18)[s - 16]
                to[pl.ds(z * ZPITCH + 2 * YPITCH + at, 8, stride=YPITCH), :] = value
            else:
                h, zb = divmod(s - 19, 3)
                base = (0, 1, 10)[h] * YPITCH + at
                if zb < 2:
                    to[pl.ds((2 + zb * 8) * ZPITCH + base, 8, stride=ZPITCH), :] = value
                else:
                    to[pl.ds(base, 1), :] = value[0:1]
                    to[pl.ds(ZPITCH + base, 1), :] = value[1:2]
                    to[pl.ds(18 * ZPITCH + base, 1), :] = value[2:3]

    sub = lax.broadcasted_iota(I32, (TILE, 128), 0)
    one = jnp.where(sub == 12, 1.0, 0.0)

    def halve(z, carry):
        for y in range(YE):
            at = pl.multiple_of(z * ZPITCH + y * YPITCH, TILE)
            for first, source, last, total in ((0, nodes_u, 12, total_u), (128, nodes_v, 9, total_v)):
                value = jnp.where(sub < last, source[pl.ds(at, TILE), :], one)
                high, low = split(value)
                tiles_h[pl.ds(at, TILE), first : first + 128] = high
                tiles_l[pl.ds(at, TILE), first : first + 128] = low
                total[pl.ds(at, TILE), :] = jnp.zeros((TILE, 128), F32)
        return carry

    lax.fori_loop(0, ZE, halve, 0)

    lane_1 = lane_ids(1)
    x_first = jnp.where((edges[2] == 0), 1, 0)
    x_last = jnp.where((edges[2] == lax.axis_size("gx") - 1), 63, 64)
    inside_x = jnp.where((lane_1 >= x_first) & (lane_1 <= x_last), 1.0, 0.0)
    y_first = jnp.where(edges[1] == 0, 1, 0)
    y_last = jnp.where(edges[1] == lax.axis_size("gy") - 1, 3, 4)
    z_first = jnp.where(edges[0] == 0, 1, 0)
    z_last = jnp.where(edges[0] == lax.axis_size("gz") - 1, 7, 8)
    left_high, left_low = big_h[...], big_l[...]

    def layer(k, carry):
        inside_z = (k >= z_first) & (k <= z_last)
        for j in range(5):
            starts = [pl.multiple_of((2 * k + r) * ZPITCH + 2 * j * YPITCH, TILE) for r in range(3)]
            high = jnp.concatenate([tiles_h[pl.ds(s, 3 * TILE), :] for s in starts], axis=0)
            low = jnp.concatenate([tiles_l[pl.ds(s, 3 * TILE), :] for s in starts], axis=0)
            both = mm3((left_high, left_low), (high, low))
            inside = inside_z & (j >= y_first) & (j <= y_last)
            coeff = jnp.where(inside, both[10:11, 0:128] * inside_x, 0.0)
            for r in range(3):
                part = slice(r * 3 * TILE, (r + 1) * 3 * TILE)
                total_u[pl.ds(starts[r], 3 * TILE), :] += both[part, 0:128] * coeff
                total_v[pl.ds(starts[r], 3 * TILE), :] += both[part, 128:256] * coeff
        return carry

    lax.fori_loop(0, 9, layer, 0)

    weave = jnp.where((lane & 1) == 0, 0, 64) + lax.shift_right_logical(lane, 1)
    low_half = lane < 64

    def finish(z, carry):
        at = (z + 2) * ZPITCH + 2 * YPITCH

        def rows(total, row):
            return total[pl.ds(at + row, 8, stride=YPITCH), :]

        def woven(e, o):
            return pick_lanes(jnp.where(low_half, e, pltpu.roll(o, 63, 1)), weave)

        held = rows(total_u, 9)
        mass = woven(pltpu.roll(held, 127, 1) + held, held)
        for c in range(3):
            where = pl.ds(pl.multiple_of((c * ZN + z) * YN, YN), YN)
            uu, vv = u[where, :], v[where, :]
            inner, image = (
                woven(pltpu.roll(rows(t, c), 127, 1) + rows(t, 6 + c), rows(t, 3 + c))
                for t in (total_u, total_v)
            )
            square = uu * uu * mass
            residual[where, :] = inner + 0.1 * square * uu - external[where, :]
            tangent[where, :] = image + 0.3 * square * vv
        return carry

    lax.fori_loop(0, ZN, finish, 0)


def contact_kernel(
    replies, quads, faces, node_x_h, node_x_l, node_y_h, node_y_l, res_in, tan_in, residual, tangent
):
    slot_faces = faces[...]
    face_ids = lax.broadcasted_iota(I32, (FACES, 128), 0) + 1
    values_h, values_l, selectors = [], [], []
    for c in range(CHUNKS):
        m = swap_groups([replies[g * CHUNKS + c] for g in range(4)])
        slot_face = slot_faces[c : c + 1]
        index = jnp.maximum(jnp.broadcast_to(slot_face, (8, 128)) - 1, 0)
        inside, outside = index & 127, index >= 128
        kin = [
            jnp.where(
                outside,
                pick_lanes(quads[pl.ds(i * 8, 8), 128:256], inside),
                pick_lanes(quads[pl.ds(i * 8, 8), 0:128], inside),
            )
            for i in range(7)
        ]

        def point(m0, m1, m2, k):
            gap = m0 + m1 * k[0] + m2 * k[1] + k[2]
            scaled = -2.0 * gap
            small = jnp.exp(-jnp.abs(scaled))
            pressure = 2.0 * (jnp.maximum(scaled, 0.0) + jnp.log1p(small))
            slope = 4.0 * jnp.where(scaled >= 0.0, 1.0, small) / (1.0 + small)
            push = slope * (m1 * k[3] + m2 * k[4] + k[5])
            return pressure * m1, pressure * m2, pressure, push * m1, push * m2, push

        main = point(m[0], m[1], m[2], kin[:6])
        last = point(m[3][0:1], m[3][1:2], m[3][2:3], [kin[6][i : i + 1] for i in range(6)])
        stack = jnp.concatenate(list(main) + list(last) + [jnp.zeros((10, 128), F32)], axis=0)
        high, low = split(stack)
        values_h.append(high)
        values_l.append(low)
        selectors.append(jnp.where(face_ids == slot_face, 1.0, 0.0).astype(BF16))
    values = jnp.concatenate(
        [jnp.concatenate(values_h, axis=1), jnp.concatenate(values_l, axis=1)], axis=0
    )
    sums = mm_nt(values, jnp.concatenate(selectors, axis=1))
    sums = sums[0:64] + sums[64:128]
    sums = jnp.concatenate([sums[:, 0:64], sums[:, 64:128], sums[:, 128:192]], axis=0)
    along = mm3(split(sums), (node_x_h[...], node_x_l[...]))
    tall = split(jnp.concatenate([along[:, i * 128 : (i + 1) * 128] for i in range(3)], axis=0))
    plane = mm3((node_y_h[...], node_y_l[...]), tall)
    for c in range(3):
        residual[c, 0] = res_in[c, 0] + plane[c * 8 : c * 8 + 8]
        tangent[c, 0] = tan_in[c, 0] + plane[24 + c * 8 : 32 + c * 8]


def call(body, outs, scratch=(), smem=(), flops=0, n=0, **more):
    specs = [
        pl.BlockSpec(memory_space=pltpu.SMEM if i in smem else pltpu.VMEM) for i in range(n)
    ]
    return pl.pallas_call(
        body,
        out_shape=tuple(jax.ShapeDtypeStruct(s, t) for s, t in outs),
        in_specs=specs,
        out_specs=tuple(pl.BlockSpec(memory_space=pltpu.VMEM) for _ in outs),
        scratch_shapes=list(scratch),
        cost_estimate=pl.CostEstimate(flops=flops, bytes_accessed=1 << 20, transcendentals=0),
        compiler_params=pltpu.CompilerParams(vmem_limit_bytes=44 << 20),
        **more,
    )


def ring(values, axis, up):
    count = lax.axis_size(axis)
    pairs = [(i, (i + 1) % count) if up else ((i + 1) % count, i) for i in range(count)]
    return lax.ppermute(values, axis, pairs)


def local(
    displacement,
    direction,
    modulus,
    external,
    stiffness,
    master_record,
    pair_face,
    pair_owner,
    pair_row,
    pair_count,
):
    u = displacement.reshape(3 * ZN * YN, XN)
    v = direction.reshape(3 * ZN * YN, XN)
    m = modulus.reshape(ZN * YN, XN)
    request, faces, z_up, z_down = call(
        request_kernel,
        [((OWNERS, 128), I32), ((CHUNKS, 128), I32), ((7, 2 * YN, XN), F32), ((7, YN, XN), F32)],
        smem=(3,), n=7, flops=1 << 20,
    )(pair_owner.reshape(8, 128), pair_row.reshape(8, 128), pair_face.reshape(8, 128), pair_count, u, v, m)
    z_low = ring(z_up, "gz", True).reshape(7 * 2 * YN, XN)
    z_high = ring(z_down, "gz", False).reshape(7 * YN, XN)
    ids = lax.all_to_all(request, GROUPS, split_axis=0, concat_axis=0, tiled=True)

    place, fixed = stiffness_places()
    first, second = face_y_map()
    constants = [jnp.asarray(x) for x in (place, *fixed, *record_map(), *face_x_map(), *first, *second)]
    y_up, y_down, big_h, big_l, table, quads = call(
        prepare_kernel,
        [
            ((7 * 2 * 24, XN), F32), ((7 * 24, XN), F32), ((BLOCK, BLOCK), BF16), ((BLOCK, BLOCK), BF16),
            ((32, ROWS), F32), ((56, 256), F32),
        ],
        n=18, flops=1 << 30,
    )(u, v, m, z_low, z_high, stiffness, master_record, *constants)
    y_low = ring(y_up, "gy", True)
    y_high = ring(y_down, "gy", False)

    (reply,) = call(gather_kernel, [((OWNERS, 8, 128), F32)], n=2, flops=1 << 20)(ids, table)
    x_up, x_down = call(edge_kernel, [((32, 128), F32), ((16, 128), F32)], n=7, flops=1 << 28)(
        u, v, m, z_low, z_high, y_low, y_high
    )
    x_low = ring(x_up, "gx", True)
    x_high = ring(x_down, "gx", False)
    replies = lax.all_to_all(reply, GROUPS, split_axis=0, concat_axis=0, tiled=True)

    edges = jnp.stack([lax.axis_index(a).astype(I32) for a in ("gz", "gy", "gx")])
    residual, tangent = call(
        element_kernel,
        [((3 * ZN * YN, XN), F32)] * 2,
        scratch=[
            pltpu.VMEM((NODE_ROWS, 128), F32),
            pltpu.VMEM((NODE_ROWS, 128), F32),
            pltpu.VMEM((NODE_ROWS, 256), BF16),
            pltpu.VMEM((NODE_ROWS, 256), BF16),
            pltpu.VMEM((NODE_ROWS, 128), F32),
            pltpu.VMEM((NODE_ROWS, 128), F32),
        ],
        smem=(0,), n=13, flops=1 << 33,
    )(
        edges, u, v, m, external.reshape(3 * ZN * YN, XN), z_low, z_high, y_low, y_high, x_low, x_high,
        big_h, big_l,
    )
    residual = residual.reshape(3, ZN, YN, XN)
    tangent = tangent.reshape(3, ZN, YN, XN)

    maps = [jnp.asarray(x) for x in (*node_x_map(), *node_y_map())]
    whole = pl.BlockSpec(memory_space=pltpu.VMEM)
    plane = pl.BlockSpec((3, 1, YN, XN), lambda i: (0, 0, 0, 0))
    out = jax.ShapeDtypeStruct((3, ZN, YN, XN), F32)
    return pl.pallas_call(
        contact_kernel,
        out_shape=(out, out),
        grid=(1,),
        in_specs=[whole] * 7 + [plane, plane],
        out_specs=(plane, plane),
        input_output_aliases={7: 0, 8: 1},
        cost_estimate=pl.CostEstimate(flops=1 << 20, bytes_accessed=1 << 20, transcendentals=0),
        compiler_params=pltpu.CompilerParams(vmem_limit_bytes=44 << 20),
    )(replies, quads, faces, *maps, residual, tangent)


def solution(mesh):
    placed = (
        P(None, "gz", "gy", "gx"),
        P(None, "gz", "gy", "gx"),
        P("gz", "gy", "gx"),
        P(None, "gz", "gy", "gx"),
        P(),
        P(None, ("gx", "gy", "gz")),
        P(("gx", "gy", "gz")),
        P(("gx", "gy", "gz"), None),
        P(("gx", "gy", "gz")),
        P(("gx", "gy", "gz")),
    )
    return jax.shard_map(
        local,
        mesh=mesh,
        in_specs=placed,
        out_specs=(P(None, "gz", "gy", "gx"), P(None, "gz", "gy", "gx")),
        check_vma=False,
    )
```

```python
import jax
import jax.numpy as jnp
import numpy as np
from jax import lax
from jax.experimental import pallas as pl
from jax.experimental.pallas import tpu as pltpu
from jax.sharding import PartitionSpec as P

F32 = jnp.float32
BF16 = jnp.bfloat16
I32 = jnp.int32

ZN, YN, XN = 16, 8, 128
ZE, YE = ZN + 3, YN + 3
OWNERS, CAP, PAIRS, ROWS = 64, 32, 1024, 2048
CHUNKS = OWNERS * CAP // 128
FACE_ROWS, FACE_COLS, FACE_LANES = 3, 63, 64
FACES = FACE_ROWS * FACE_LANES
SLABS = 28
TILE = 16
YPITCH = TILE
ZPITCH = YE * TILE
NODE_ROWS = ZE * ZPITCH
BLOCK = 9 * TILE
GROUPS = ("gx", "gy")
GROUP = 14
GATHERED = 16


def shapes_1d():
    points = np.array([-np.sqrt(0.6), 0.0, np.sqrt(0.6)])
    gauss = np.array([5.0, 8.0, 5.0]) / 9.0
    line = np.stack(
        [points * (points - 1.0) / 2.0, 1.0 - points * points, points * (points + 1.0) / 2.0],
        axis=1,
    )
    return line, gauss


def halves(values):
    high = np.asarray(values, np.float32).astype(jnp.bfloat16)
    low = (np.asarray(values, np.float64) - high.astype(np.float64)).astype(jnp.bfloat16)
    return high, low


def record_map():
    line, _ = shapes_1d()
    out = np.zeros((32, 27))
    for k in range(3):
        for qy in range(3):
            for qx in range(3):
                q = 3 * qy + qx
                row = k * 8 + q if q < 8 else 24 + k
                for b in range(3):
                    for a in range(3):
                        out[row, 9 * k + 3 * b + a] = line[qy, b] * line[qx, a]
    return halves(out)


def quad_row(part, q):
    return part * 8 + q if q < 8 else 48 + part


def face_x_map():
    line, _ = shapes_1d()
    out = np.zeros((128, 6 * 128))
    for qx in range(3):
        for side in range(2):
            for fx in range(FACE_COLS):
                for a in range(3):
                    out[2 * fx + a, (2 * qx + side) * 128 + side * 64 + fx] = line[qx, a]
    return halves(out)


def face_y_map():
    line, _ = shapes_1d()
    first = np.zeros((56, 6 * 48))
    second = np.zeros((56, 6 * 48))
    for part in range(6):
        for qy in range(3):
            for qx in range(3):
                row = quad_row(part, 3 * qy + qx)
                for b in range(3):
                    first[row, (2 * qx) * 48 + part * 8 + b] = line[qy, b]
                    first[row, (2 * qx + 1) * 48 + part * 8 + 2 + b] = line[qy, b]
                    second[row, (2 * qx) * 48 + part * 8 + 4 + b] = line[qy, b]
    return halves(first), halves(second)


def node_x_map():
    line, _ = shapes_1d()
    out = np.zeros((FACE_LANES, 3 * 128))
    for qx in range(3):
        for fx in range(FACE_COLS):
            for a in range(3):
                out[fx, qx * 128 + 2 * fx + a] = line[qx, a]
    return halves(out)


def node_y_map():
    line, gauss = shapes_1d()
    out = np.zeros((48, 3 * FACE_ROWS * 64))
    for part in range(6):
        for qx in range(3):
            for qy in range(3):
                weight = 0.25 * gauss[qx] * gauss[qy] * (-1.0 if part < 3 else 1.0)
                for fy in range(FACE_ROWS):
                    for b in range(3):
                        column = qx * FACE_ROWS * 64 + fy * 64 + quad_row(part, 3 * qy + qx)
                        out[part * 8 + 2 * fy + b, column] = weight * line[qy, b]
    return halves(out)


def stiffness_places():
    place = np.zeros((BLOCK, 81))
    for block in range(9):
        for p in range(3):
            for c in range(3):
                place[block * TILE + 3 * p + c, block * 9 + 3 * p + c] = 1.0
    fixed = np.zeros((BLOCK, BLOCK))
    for block in range(9):
        fixed[block * TILE + 9, block * TILE + 12] = 1.0
        for p in range(3):
            fixed[10, block * TILE + 9 + p] = 1.0 / 27.0
    fixed[[b * TILE + 9 for b in range(1, 9)], :] = 0.0
    for block in range(1, 9):
        fixed[block * TILE + 9, block * TILE + 12] = 1.0
    return place.astype(np.float32), halves(fixed)


def packed(pieces, rows, columns):
    out = np.zeros((rows, columns), jnp.bfloat16)
    for row, column, piece in pieces:
        out[row : row + piece.shape[0], column : column + piece.shape[1]] = piece
    return out


def prepare_constants():
    place, fixed = stiffness_places()
    record, along = record_map(), face_x_map()
    first, second = face_y_map()
    pieces = [
        (0, 0, along[0]), (128, 0, along[1]),
        (256, 0, first[0]), (256, 384, second[0]), (320, 0, first[1]), (320, 384, second[1]),
        (384, 0, fixed[0]), (384, 256, fixed[1]), (384, 512, place.astype(jnp.bfloat16)),
        (528, 0, record[0]), (528, 128, record[1]),
    ]
    return packed(pieces, 560, 768)


def contact_constants():
    along, across = node_x_map(), node_y_map()
    pieces = [(0, 0, along[0]), (64, 0, along[1]), (128, 0, across[0]), (176, 0, across[1])]
    return packed(pieces, 224, 576)


def split(values):
    high = values.astype(BF16)
    return high, (values - high.astype(F32)).astype(BF16)


def mm(a, b):
    return jnp.dot(a, b, preferred_element_type=F32)


def mm_nt(a, b):
    return lax.dot_general(a, b, (((1,), (1,)), ((), ())), preferred_element_type=F32)


def mm3(a, b):
    return mm(a[0], b[0]) + (mm(a[0], b[1]) + mm(a[1], b[0]))


def lane_ids(rows):
    return lax.broadcasted_iota(I32, (rows, 128), 1)


def pick_lanes(values, index):
    return jnp.take_along_axis(values, index, axis=1, mode="promise_in_bounds")


def compact(values):
    return (
        values[0:16]
        + pltpu.roll(values[16:32], 32, 1)
        + pltpu.roll(values[32:48], 64, 1)
        + pltpu.roll(values[48:64], 96, 1)
    )


def by_group(lane, parts):
    odd = (lane & 32) != 0
    return jnp.where(lane < 64, jnp.where(odd, parts[1], parts[0]), jnp.where(odd, parts[3], parts[2]))


def swap_groups(quads):
    lane = lane_ids(8)
    moved = [[by_group(lane, [q[(g + r) % 4] for g in range(4)]) for q in quads] for r in range(4)]
    for r in range(1, 4):
        moved[r] = [pltpu.roll(x, 32 * r, 1) for x in moved[r]]
    return [
        [by_group(lane, [moved[(f - g) % 4][i] for f in range(4)]) for g in range(4)]
        for i in range(len(quads))
    ]


def request_kernel(owner, row, face, count, u, v, m, request, faces, z_up, z_down, arrived):
    layers = []
    for i, (to, start, size) in enumerate(((z_up, ZN - 2, 2), (z_down, 0, 1))):
        part = pl.ds(start, size)
        layers += [
            pltpu.make_async_copy(u.at[:, part], to.at[pl.ds(0, 3)], arrived.at[3 * i]),
            pltpu.make_async_copy(v.at[:, part], to.at[pl.ds(3, 3)], arrived.at[3 * i + 1]),
            pltpu.make_async_copy(m.at[part], to.at[6], arrived.at[3 * i + 2]),
        ]
    for copy in layers:
        copy.start()
    live_count = count[0]
    who = lax.broadcasted_iota(I32, (OWNERS, 128), 0)
    lane = lane_ids(1)
    hits = []
    for t in range(PAIRS // 128):
        live = lane + t * 128 < live_count
        target = jnp.where(live, owner[pl.ds(t, 1), :], -1)
        hits.append(jnp.where(who == target, 1.0, 0.0).astype(F32))
    before = jnp.where(
        lax.broadcasted_iota(I32, (128, 128), 0) < lax.broadcasted_iota(I32, (128, 128), 1), 1.0, 0.0
    ).astype(BF16)
    ranks = mm(jnp.concatenate([h.astype(BF16) for h in hits], axis=0), before)
    base = jnp.zeros((OWNERS, 1), F32)
    places = lax.broadcasted_iota(I32, (128, 128), 0)
    highs, lows, sides = [], [], []
    for t in range(PAIRS // 128):
        rank = jnp.sum(hits[t] * (ranks[t * OWNERS : (t + 1) * OWNERS] + base), axis=0, keepdims=True)
        base = base + jnp.sum(hits[t], axis=1, keepdims=True)
        here = places == rank.astype(I32)
        number = row[pl.ds(t, 1), :] + 1
        f = face[pl.ds(t, 1), :]
        f = f + jnp.where(f >= FACE_COLS, 1, 0) + jnp.where(f >= 2 * FACE_COLS, 1, 0) + 1
        highs.append(jnp.where(here, lax.shift_right_logical(number, 6).astype(F32), 0.0).astype(BF16))
        lows.append(jnp.where(here, (number & 63).astype(F32), 0.0).astype(BF16))
        sides.append(jnp.where(here, f.astype(F32), 0.0).astype(BF16))
    hit = jnp.concatenate([h.astype(BF16) for h in hits], axis=1)
    high = mm_nt(hit, jnp.concatenate(highs, axis=1))
    low = mm_nt(hit, jnp.concatenate(lows, axis=1))
    request[...] = (high * 64.0 + low).astype(I32)
    faces[...] = compact(mm_nt(hit, jnp.concatenate(sides, axis=1))).astype(I32)
    for copy in layers:
        copy.wait()


def side_kernel(u, v, m, z_low, z_high, y_up, y_down):
    for first, field, comps in ((0, u, 3), (3, v, 3), (6, m, 1)):
        for c in range(comps):
            n = first + c
            for out, h, y in ((y_up, 0, YN - 2), (y_up, 1, YN - 1), (y_down, 0, 0)):
                at = (n * (2 if out is y_up else 1) + h) * 24
                out[pl.ds(at, ZN), :] = field[pl.ds(c * ZN * YN + y, ZN, stride=YN), :]
                out[pl.ds(at + 16, 8), :] = jnp.zeros((8, 128), F32)
                out[pl.ds(at + 16, 1), :] = z_low[pl.ds((n * 2) * YN + y, 1), :]
                out[pl.ds(at + 17, 1), :] = z_low[pl.ds((n * 2 + 1) * YN + y, 1), :]
                out[pl.ds(at + 18, 1), :] = z_high[pl.ds(n * YN + y, 1), :]


def prepare_kernel(u, v, stiffness, master, fixed, big_h, big_l, table, quads):
    places = fixed[384:528, 512:593]
    high, low = split(stiffness[...])
    lower = (stiffness[...] - high.astype(F32) - low.astype(F32)).astype(BF16)
    spread = [mm_nt(mm(places, part).astype(BF16), places) for part in (high, low, lower)]
    high, low = split((spread[0] + spread[1]) + spread[2])
    big_h[...] = high + fixed[384:528, 0:144]
    big_l[...] = low + fixed[384:528, 256:400]
    table[...] = mm3((fixed[528:560, 0:27], fixed[528:560, 128:155]), split(master[...]))
    plane = jnp.concatenate(
        [field[pl.ds(c * ZN * YN, YN), :] for field in (u, v) for c in range(3)], axis=0
    )
    wide = mm3(split(plane), (fixed[0:128, :], fixed[128:256, :]))
    tall = split(jnp.concatenate([wide[:, i * 128 : (i + 1) * 128] for i in range(6)], axis=0))
    for first, to in ((0, 0), (384, 128)):
        pair = fixed[256:312, first : first + 288], fixed[320:376, first : first + 288]
        quads[:, to : to + 128] = mm3(pair, tall)


def gather_kernel(ids, table, reply):
    numbers = jnp.maximum(compact(ids[...]) - 1, 0)
    for base in range(0, CHUNKS, GATHERED):
        found = []
        for c in range(base, base + GATHERED):
            number = jnp.broadcast_to(numbers[c : c + 1], (8, 128))
            inside = number & 127
            outside = lax.shift_right_logical(number, 7)
            parts = []
            for f in range(4):
                total = pick_lanes(table[pl.ds(f * 8, 8), 0:128], inside)
                for k in range(1, ROWS // 128):
                    piece = pick_lanes(table[pl.ds(f * 8, 8), k * 128 : (k + 1) * 128], inside)
                    total = jnp.where(outside == k, piece, total)
                parts.append(total)
            found.append(parts)
        tiles = swap_groups(found)
        for i in range(GATHERED):
            for g in range(4):
                reply[g * CHUNKS + base + i] = tiles[i][g]


def slab(fields, halos, n, s):
    z_low, z_high, y_low, y_high = halos
    if s < 16:
        return fields[n // 3][pl.ds((n % 3 * ZN + s) * YN, YN), :]
    if s < 18:
        return z_low[pl.ds((n * 2 + s - 16) * YN, YN), :]
    if s < 19:
        return z_high[pl.ds(n * YN, YN), :]
    h, zb = divmod(s - 19, 3)
    if h < 2:
        return y_low[pl.ds((n * 2 + h) * 24 + zb * 8, 8), :]
    return y_high[pl.ds(n * 24 + zb * 8, 8), :]


def edge_kernel(u, v, m, z_low, z_high, y_low, y_high, x_down):
    fields, halos = (u, v, m), (z_low, z_high, y_low, y_high)
    lane = lane_ids(8)
    down = [jnp.zeros((8, 128), F32) for _ in range(2)]
    for c in range(4):
        for s in range(SLABS):
            k, spot = divmod(c * SLABS + s, 64)
            one = slab(fields, halos, 6 if c == 3 else c, s)
            two = one if c == 3 else slab(fields, halos, 3 + c, s)
            one = pltpu.roll(one, spot, 1) if spot else one
            two = pltpu.roll(two, 64 + spot, 1)
            down[k] = jnp.where(lane == spot, one, jnp.where(lane == 64 + spot, two, down[k]))
    for k in range(2):
        x_down[pl.ds(k * 8, 8), :] = down[k]


def element_kernel(
    edges, u, v, m, external, z_low, z_high, y_low, y_high, x_high, big_h, big_l,
    residual, tangent, last, nodes, tiles_h, tiles_l, total,
):
    fields, halos = (u, v, m), (z_low, z_high, y_low, y_high)
    lane = lane_ids(8)
    low_half = lane < 64
    spot_of = lane & 63
    at_last = spot_of == 63
    even_even = 2 * spot_of
    odd_odd = 2 * spot_of + 1
    next_next = (2 * spot_of + 2) & 127

    def node_values(group):
        ones = [slab(fields, halos, 6 if c == 3 else c, s) for c, s in group]
        twos = [None if c == 3 else slab(fields, halos, 3 + c, s) for c, s in group]
        found = []
        for index in (even_even, odd_odd, next_next):
            first = [pick_lanes(one, index) for one in ones]
            second = [None if two is None else pick_lanes(two, index) for two in twos]
            found.append([a if b is None else jnp.where(low_half, a, b) for a, b in zip(first, second)])
        for i, (c, s) in enumerate(group):
            k, spot = divmod(c * SLABS + s, 64)
            held = x_high[pl.ds(k * 8, 8), :]
            after = held if spot == 63 else pltpu.roll(held, 63 - spot, 1)
            found[2][i] = jnp.where(at_last, after, found[2][i])
        return list(zip(*found))

    def put(value, s, at):
        if s < 19:
            z = s + 2 if s < 16 else (0, 1, 18)[s - 16]
            nodes[pl.ds(z * ZPITCH + 2 * YPITCH + at, 8, stride=YPITCH), :] = value
            return
        h, zb = divmod(s - 19, 3)
        base = (0, 1, 10)[h] * YPITCH + at
        if zb < 2:
            nodes[pl.ds((2 + zb * 8) * ZPITCH + base, 8, stride=ZPITCH), :] = value
        else:
            nodes[pl.ds(base, 1), :] = value[0:1]
            nodes[pl.ds(ZPITCH + base, 1), :] = value[1:2]
            nodes[pl.ds(18 * ZPITCH + base, 1), :] = value[2:3]

    todo = [(c, s) for c in range(4) for s in range(SLABS)]
    for start in range(0, len(todo), GROUP):
        group = todo[start : start + GROUP]
        values = node_values(group)
        for (c, s), three in zip(group, values):
            first, step = (9, 1) if c == 3 else (c, 3)
            for p in range(3):
                put(three[p], s, first + step * p)

    sub = lax.broadcasted_iota(I32, (TILE, 128), 0)
    one = jnp.where(sub == 12, 1.0, 0.0)

    def halve(z, carry):
        places = [pl.ds(pl.multiple_of(z * ZPITCH + y * YPITCH, TILE), TILE) for y in range(YE)]
        pairs = [split(jnp.where(sub < 12, nodes[at, :], one)) for at in places]
        for at, (high, low) in zip(places, pairs):
            tiles_h[at, :] = high
            tiles_l[at, :] = low
        return carry

    lax.fori_loop(0, ZE, halve, 0)

    x_last = jnp.where(edges[2] == lax.axis_size("gx") - 1, 63, 64)
    inside_x = jnp.where((lane_ids(1) & 63) < x_last, 1.0, 0.0)
    y_first = jnp.where(edges[1] == 0, 1, 0)
    y_last = jnp.where(edges[1] == lax.axis_size("gy") - 1, 3, 4)
    z_first = jnp.where(edges[0] == 0, 1, 0)
    z_last = jnp.where(edges[0] == lax.axis_size("gz") - 1, 7, 8)
    left_high, left_low = big_h[...], big_l[...]

    total[pl.ds(0, ZPITCH), :] = jnp.zeros((ZPITCH, 128), F32)

    def inside_of(k, j):
        return (k >= z_first) & (k <= z_last) & (j >= y_first) & (j <= y_last)

    def products(elements):
        operands = []
        for tiles in (tiles_h, tiles_l):
            columns = []
            for k, j in elements:
                starts = [pl.multiple_of((2 * k + r) * ZPITCH + 2 * j * YPITCH, TILE) for r in range(3)]
                columns.append(jnp.concatenate([tiles[pl.ds(a, 3 * TILE), :] for a in starts], axis=0))
            operands.append(jnp.concatenate(columns, axis=1))
        both = mm3((left_high, left_low), operands)
        forces = []
        for i, (k, j) in enumerate(elements):
            mine = both[:, i * 128 : (i + 1) * 128]
            forces.append(mine * jnp.where(inside_of(k, j), mine[10:11] * inside_x, 0.0))
        return forces

    def part(force, r, q):
        return force[(3 * r + q) * TILE : (3 * r + q + 1) * TILE]

    def place_of(z, y):
        return pl.ds(pl.multiple_of(z * ZPITCH + y * YPITCH, TILE), TILE)

    def layers(i, carry):
        shared = None
        for j in range(5):
            one, two = products([(2 * i, j), (2 * i + 1, j)])
            for q in range(3):
                sums = [part(one, 0, q), part(one, 1, q), part(one, 2, q) + part(two, 0, q), part(two, 1, q), part(two, 2, q)]
                if q == 0 and shared is not None:
                    sums = [a + b for a, b in zip(sums, shared)]
                if q == 2 and j < 4:
                    shared = sums
                    continue
                y = 2 * j + q
                sums[0] = sums[0] + total[place_of(4 * i, y), :]
                for r in range(5):
                    total[place_of(4 * i + r, y), :] = sums[r]
        return carry

    lax.fori_loop(0, 4, layers, 0)
    last_layer = products([(8, 0), (8, 1)]) + products([(8, 2), (8, 3)]) + products([(8, 4)])
    for r in range(3):
        for y in range(YE):
            held = [part(last_layer[j], r, y - 2 * j) for j in range(5) if 0 <= y - 2 * j <= 2]
            held = held + [total[place_of(16, y), :]] if r == 0 else held
            total[place_of(16 + r, y), :] = sum(held[1:], held[0])

    half = lax.shift_right_logical(lane, 1)
    weave_u = half + jnp.where((lane & 1) == 0, 0, 64)
    weave_v = half + jnp.where((lane & 1) == 0, 64, 0)
    at_first = spot_of == 0
    sent = jnp.zeros((8, 128), F32)
    for start in range(0, ZN, 4):
        layer = range(start, start + 4)

        def rows(z, row):
            return total[pl.ds((z + 2) * ZPITCH + 2 * YPITCH + row, 8, stride=YPITCH), :]

        held = [rows(z, 9) for z in layer]
        p0 = [rows(z, c) for z in layer for c in range(3)]
        p1 = [rows(z, 3 + c) for z in layer for c in range(3)]
        p2 = [rows(z, 6 + c) for z in layer for c in range(3)]
        after = [pltpu.roll(x, 1, 1) for x in held + p2]
        odd = [pltpu.roll(x, 64, 1) for x in p1]
        for i, z in enumerate(layer):
            sent = jnp.where(spot_of == 48 + z, pltpu.roll(held[i], (z - 15) % 128, 1), sent)
            for c in range(3):
                moved = pltpu.roll(p2[3 * i + c], (c * 16 + z - 63) % 128, 1)
                sent = jnp.where(spot_of == c * 16 + z, moved, sent)
        after = [jnp.where(at_first, 0.0, x) for x in after]
        even = [a + b for a, b in zip(p0, after[4:])]
        mass = [pick_lanes(jnp.where(low_half, a + b, a), weave_u) for a, b in zip(held, after)]
        inner = [pick_lanes(jnp.where(low_half, a, b), weave_u) for a, b in zip(even, odd)]
        image = [pick_lanes(jnp.where(low_half, b, a), weave_v) for a, b in zip(even, odd)]
        results = []
        for i, z in enumerate(layer):
            for c in range(3):
                where = pl.ds((c * ZN + z) * YN, YN)
                uu, vv = u[where, :], v[where, :]
                square = uu * uu * mass[i]
                results.append(
                    (
                        where,
                        inner[3 * i + c] + 0.1 * square * uu - external[where, :],
                        image[3 * i + c] + 0.3 * square * vv,
                    )
                )
        for where, res, tan in results:
            residual[where, :] = res
            tangent[where, :] = tan
    last[...] = sent


def slot_kernel(quads, faces, kin, selector):
    slot_faces = faces[...]
    face_ids = lax.broadcasted_iota(I32, (FACES, 128), 0) + 1
    for c in range(CHUNKS):
        slot_face = slot_faces[c : c + 1]
        index = jnp.maximum(jnp.broadcast_to(slot_face, (8, 128)) - 1, 0)
        inside, outside = index & 127, index >= 128
        for i in range(7):
            kin[c, pl.ds(i * 8, 8), :] = jnp.where(
                outside,
                pick_lanes(quads[pl.ds(i * 8, 8), 128:256], inside),
                pick_lanes(quads[pl.ds(i * 8, 8), 0:128], inside),
            )
        selector[:, c * 128 : (c + 1) * 128] = jnp.where(face_ids == slot_face, 1.0, 0.0).astype(BF16)


def contact_kernel(replies, kin, selector, fixed, left, u, v, res_in, tan_in, residual, tangent):
    values_h, values_l = [], []
    records = swap_groups([[replies[g * CHUNKS + c] for g in range(4)] for c in range(CHUNKS)])
    for c in range(CHUNKS):
        m = records[c]

        def point(m0, m1, m2, k):
            gap = m0 + m1 * k[0] + m2 * k[1] + k[2]
            scaled = -2.0 * gap
            small = jnp.exp(-jnp.abs(scaled))
            pressure = 2.0 * (jnp.maximum(scaled, 0.0) + jnp.log1p(small))
            slope = 4.0 * jnp.where(scaled >= 0.0, 1.0, small) / (1.0 + small)
            push = slope * (m1 * k[3] + m2 * k[4] + k[5])
            return pressure * m1, pressure * m2, pressure, push * m1, push * m2, push

        main = point(m[0], m[1], m[2], [kin[c, pl.ds(i * 8, 8), :] for i in range(6)])
        ends = kin[c, pl.ds(48, 8), :]
        ninth = point(m[3][0:1], m[3][1:2], m[3][2:3], [ends[i : i + 1] for i in range(6)])
        stack = jnp.concatenate(list(main) + list(ninth) + [jnp.zeros((10, 128), F32)], axis=0)
        high, low = split(stack)
        values_h.append(high)
        values_l.append(low)
    values = jnp.concatenate(
        [jnp.concatenate(values_h, axis=1), jnp.concatenate(values_l, axis=1)], axis=0
    )
    sums = mm_nt(values, selector[...])
    sums = sums[0:64] + sums[64:128]
    sums = jnp.concatenate([sums[:, 0:64], sums[:, 64:128], sums[:, 128:192]], axis=0)
    along = mm3(split(sums), (fixed[0:64, 0:384], fixed[64:128, 0:384]))
    tall = split(jnp.concatenate([along[:, i * 128 : (i + 1) * 128] for i in range(3)], axis=0))
    plane = mm3((fixed[128:176, :], fixed[176:224, :]), tall)
    at_first = lane_ids(8) == 0
    came = left[...]
    for z in range(ZN):
        mass = pltpu.roll(came, 80 - z, 1)
        for c in range(3):
            where = pl.ds((c * ZN + z) * YN, YN)
            uu, vv = u[where, :], v[where, :]
            square = uu * uu * mass
            spot = c * 16 + z
            inner = came if spot == 0 else pltpu.roll(came, 128 - spot, 1)
            image = pltpu.roll(came, 64 - spot, 1)
            res = res_in[where, :] + jnp.where(at_first, inner + 0.1 * square * uu, 0.0)
            tan = tan_in[where, :] + jnp.where(at_first, image + 0.3 * square * vv, 0.0)
            if z == 0:
                res = res + plane[c * 8 : c * 8 + 8]
                tan = tan + plane[24 + c * 8 : 32 + c * 8]
            residual[where, :] = res
            tangent[where, :] = tan


def call(body, outs, scratch=(), smem=(), hbm=(), flops=0, n=0, limit=44, **more):
    places = [pltpu.SMEM if i in smem else pl.ANY if i in hbm else pltpu.VMEM for i in range(n)]
    specs = [pl.BlockSpec(memory_space=place) for place in places]
    return pl.pallas_call(
        body,
        out_shape=tuple(jax.ShapeDtypeStruct(s, t) for s, t in outs),
        in_specs=specs,
        out_specs=tuple(pl.BlockSpec(memory_space=pltpu.VMEM) for _ in outs),
        scratch_shapes=list(scratch),
        cost_estimate=pl.CostEstimate(flops=flops, bytes_accessed=0, transcendentals=0),
        compiler_params=pltpu.CompilerParams(vmem_limit_bytes=limit << 20),
        **more,
    )


def ring(values, axis, up):
    count = lax.axis_size(axis)
    pairs = [(i, (i + 1) % count) if up else ((i + 1) % count, i) for i in range(count)]
    return lax.ppermute(values, axis, pairs)


def local(
    displacement,
    direction,
    modulus,
    external,
    stiffness,
    master_record,
    pair_face,
    pair_owner,
    pair_row,
    pair_count,
):
    u = displacement.reshape(3 * ZN * YN, XN)
    v = direction.reshape(3 * ZN * YN, XN)
    m = modulus.reshape(ZN * YN, XN)
    request, faces, z_up, z_down = call(
        request_kernel,
        [((OWNERS, 128), I32), ((CHUNKS, 128), I32), ((7, 2, YN, XN), F32), ((7, 1, YN, XN), F32)],
        scratch=[pltpu.SemaphoreType.DMA((6,))], smem=(3,), hbm=(4, 5, 6), n=7, limit=63,
    )(
        pair_owner.reshape(8, 128), pair_row.reshape(8, 128), pair_face.reshape(8, 128), pair_count,
        displacement, direction, modulus,
    )
    z_low = ring(z_up, "gz", True).reshape(7 * 2 * YN, XN)
    z_high = ring(z_down, "gz", False).reshape(7 * YN, XN)
    ids = lax.all_to_all(request, GROUPS, split_axis=0, concat_axis=0, tiled=True)

    big_h, big_l, table, quads = call(
        prepare_kernel,
        [((BLOCK, BLOCK), BF16), ((BLOCK, BLOCK), BF16), ((32, ROWS), F32), ((56, 256), F32)],
        n=5,
    )(u, v, stiffness, master_record, jnp.asarray(prepare_constants()))
    kin, selector = call(
        slot_kernel, [((CHUNKS, 56, 128), F32), ((FACES, OWNERS * CAP), BF16)], n=2
    )(quads, faces)
    y_up, y_down = call(side_kernel, [((7 * 2 * 24, XN), F32), ((7 * 24, XN), F32)], n=5)(
        u, v, m, z_low, z_high
    )
    y_low = ring(y_up, "gy", True)
    y_high = ring(y_down, "gy", False)

    (reply,) = call(gather_kernel, [((OWNERS, 8, 128), F32)], n=2, flops=1 << 20)(ids, table)
    (x_down,) = call(edge_kernel, [((16, 128), F32)], n=7)(u, v, m, z_low, z_high, y_low, y_high)
    x_high = ring(x_down, "gx", False)
    replies = lax.all_to_all(reply, GROUPS, split_axis=0, concat_axis=0, tiled=True)

    edges = jnp.stack([lax.axis_index(a).astype(I32) for a in ("gz", "gy", "gx")])
    residual, tangent, last = call(
        element_kernel,
        [((3 * ZN * YN, XN), F32), ((3 * ZN * YN, XN), F32), ((8, 128), F32)],
        scratch=[
            pltpu.VMEM((NODE_ROWS, 128), F32),
            pltpu.VMEM((NODE_ROWS, 128), BF16),
            pltpu.VMEM((NODE_ROWS, 128), BF16),
            pltpu.VMEM((NODE_ROWS, 128), F32),
        ],
        smem=(0,), n=12, flops=1 << 33,
    )(
        edges, u, v, m, external.reshape(3 * ZN * YN, XN), z_low, z_high, y_low, y_high, x_high,
        big_h, big_l,
    )
    left = ring(last, "gx", True)
    residual, tangent = call(
        contact_kernel, [((3 * ZN * YN, XN), F32), ((3 * ZN * YN, XN), F32)], n=9, flops=1 << 20
    )(replies, kin, selector, jnp.asarray(contact_constants()), left, u, v, residual, tangent)
    return residual.reshape(3, ZN, YN, XN), tangent.reshape(3, ZN, YN, XN)


def solution(mesh):
    placed = (
        P(None, "gz", "gy", "gx"),
        P(None, "gz", "gy", "gx"),
        P("gz", "gy", "gx"),
        P(None, "gz", "gy", "gx"),
        P(),
        P(None, ("gx", "gy", "gz")),
        P(("gx", "gy", "gz")),
        P(("gx", "gy", "gz"), None),
        P(("gx", "gy", "gz")),
        P(("gx", "gy", "gz")),
    )
    return jax.shard_map(
        local,
        mesh=mesh,
        in_specs=placed,
        out_specs=(P(None, "gz", "gy", "gx"), P(None, "gz", "gy", "gx")),
        check_vma=False,
    )
```

```python
import jax
import jax.numpy as jnp
import numpy as np
from jax import lax
from jax.experimental import pallas as pl
from jax.experimental.pallas import tpu as pltpu
from jax.sharding import PartitionSpec as P

F32 = jnp.float32
BF16 = jnp.bfloat16
I32 = jnp.int32

ZN, YN, XN = 16, 8, 128
ZE, YE = ZN + 3, YN + 3
OWNERS, CAP, PAIRS, ROWS = 64, 32, 1024, 2048
CHUNKS = OWNERS * CAP // 128
FACE_ROWS, FACE_COLS, FACE_LANES = 3, 63, 64
FACES = FACE_ROWS * FACE_LANES
SLABS = 28
TILE = 16
YPITCH = TILE
ZPITCH = YE * TILE
NODE_ROWS = ZE * ZPITCH
BLOCK = 9 * TILE
GROUPS = ("gx", "gy")
GROUP = 14


def shapes_1d():
    points = np.array([-np.sqrt(0.6), 0.0, np.sqrt(0.6)])
    gauss = np.array([5.0, 8.0, 5.0]) / 9.0
    line = np.stack(
        [points * (points - 1.0) / 2.0, 1.0 - points * points, points * (points + 1.0) / 2.0],
        axis=1,
    )
    return line, gauss


def halves(values):
    high = np.asarray(values, np.float32).astype(jnp.bfloat16)
    low = (np.asarray(values, np.float64) - high.astype(np.float64)).astype(jnp.bfloat16)
    return high, low


def record_map():
    line, _ = shapes_1d()
    out = np.zeros((32, 27))
    for k in range(3):
        for qy in range(3):
            for qx in range(3):
                q = 3 * qy + qx
                row = k * 8 + q if q < 8 else 24 + k
                for b in range(3):
                    for a in range(3):
                        out[row, 9 * k + 3 * b + a] = line[qy, b] * line[qx, a]
    return halves(out)


def quad_row(part, q):
    return part * 8 + q if q < 8 else 48 + part


def face_x_map():
    line, _ = shapes_1d()
    out = np.zeros((128, 6 * 128))
    for qx in range(3):
        for side in range(2):
            for fx in range(FACE_COLS):
                for a in range(3):
                    out[2 * fx + a, (2 * qx + side) * 128 + side * 64 + fx] = line[qx, a]
    return halves(out)


def face_y_map():
    line, _ = shapes_1d()
    first = np.zeros((56, 6 * 48))
    second = np.zeros((56, 6 * 48))
    for part in range(6):
        for qy in range(3):
            for qx in range(3):
                row = quad_row(part, 3 * qy + qx)
                for b in range(3):
                    first[row, (2 * qx) * 48 + part * 8 + b] = line[qy, b]
                    first[row, (2 * qx + 1) * 48 + part * 8 + 2 + b] = line[qy, b]
                    second[row, (2 * qx) * 48 + part * 8 + 4 + b] = line[qy, b]
    return halves(first), halves(second)


def node_x_map():
    line, _ = shapes_1d()
    out = np.zeros((FACE_LANES, 3 * 128))
    for qx in range(3):
        for fx in range(FACE_COLS):
            for a in range(3):
                out[fx, qx * 128 + 2 * fx + a] = line[qx, a]
    return halves(out)


def node_y_map():
    line, gauss = shapes_1d()
    out = np.zeros((48, 3 * FACE_ROWS * 64))
    for part in range(6):
        for qx in range(3):
            for qy in range(3):
                weight = 0.25 * gauss[qx] * gauss[qy] * (-1.0 if part < 3 else 1.0)
                for fy in range(FACE_ROWS):
                    for b in range(3):
                        column = qx * FACE_ROWS * 64 + fy * 64 + quad_row(part, 3 * qy + qx)
                        out[part * 8 + 2 * fy + b, column] = weight * line[qy, b]
    return halves(out)


def stiffness_places():
    place = np.zeros((BLOCK, 81))
    for block in range(9):
        for p in range(3):
            for c in range(3):
                place[block * TILE + 3 * p + c, block * 9 + 3 * p + c] = 1.0
    fixed = np.zeros((BLOCK, BLOCK))
    for block in range(9):
        fixed[block * TILE + 9, block * TILE + 12] = 1.0
        for p in range(3):
            fixed[10, block * TILE + 9 + p] = 1.0 / 27.0
    fixed[[b * TILE + 9 for b in range(1, 9)], :] = 0.0
    for block in range(1, 9):
        fixed[block * TILE + 9, block * TILE + 12] = 1.0
    return place.astype(np.float32), halves(fixed)


def packed(pieces, rows, columns):
    out = np.zeros((rows, columns), jnp.bfloat16)
    for row, column, piece in pieces:
        out[row : row + piece.shape[0], column : column + piece.shape[1]] = piece
    return out


def element_constants():
    place, fixed = stiffness_places()
    return packed([(0, 0, fixed[0]), (0, 256, fixed[1]), (0, 512, place.astype(jnp.bfloat16))], 144, 640)


def slot_constants():
    along = face_x_map()
    first, second = face_y_map()
    pieces = [
        (0, 0, along[0]), (128, 0, along[1]),
        (256, 0, first[0]), (256, 384, second[0]), (320, 0, first[1]), (320, 384, second[1]),
    ]
    return packed(pieces, 384, 768)


def table_constants():
    high, low = record_map()
    return packed([(0, 0, high), (0, 128, low)], 32, 256)


def contact_constants():
    along, across = node_x_map(), node_y_map()
    pieces = [(0, 0, along[0]), (64, 0, along[1]), (128, 0, across[0]), (176, 0, across[1])]
    return packed(pieces, 224, 576)


def split(values):
    high = values.astype(BF16)
    return high, (values - high.astype(F32)).astype(BF16)


def mm(a, b):
    return jnp.dot(a, b, preferred_element_type=F32)


def mm_nt(a, b):
    return lax.dot_general(a, b, (((1,), (1,)), ((), ())), preferred_element_type=F32)


def mm3(a, b):
    return mm(a[0], b[0]) + (mm(a[0], b[1]) + mm(a[1], b[0]))


def lane_ids(rows):
    return lax.broadcasted_iota(I32, (rows, 128), 1)


def pick_lanes(values, index):
    return jnp.take_along_axis(values, index, axis=1, mode="promise_in_bounds")


def compact(values):
    return (
        values[0:16]
        + pltpu.roll(values[16:32], 32, 1)
        + pltpu.roll(values[32:48], 64, 1)
        + pltpu.roll(values[48:64], 96, 1)
    )


def by_group(lane, parts):
    odd = (lane & 32) != 0
    return jnp.where(lane < 64, jnp.where(odd, parts[1], parts[0]), jnp.where(odd, parts[3], parts[2]))


def swap_groups(quads):
    lane = lane_ids(8)
    moved = [[by_group(lane, [q[(g + r) % 4] for g in range(4)]) for q in quads] for r in range(4)]
    for r in range(1, 4):
        moved[r] = [pltpu.roll(x, 32 * r, 1) for x in moved[r]]
    return [
        [by_group(lane, [moved[(f - g) % 4][i] for f in range(4)]) for g in range(4)]
        for i in range(len(quads))
    ]


def request_kernel(
    owners, rows, sides_in, counts, u, v, m, request, faces, z_up, z_down,
    owner, row, face, arrived,
):
    first = [
        pltpu.make_async_copy(source, to, arrived.at[6 + i])
        for i, (source, to) in enumerate(((owners, owner), (rows, row), (sides_in, face)))
    ]
    for copy in first:
        copy.start()
    layers = []
    for i, (to, start, size) in enumerate(((z_up, ZN - 2, 2), (z_down, 0, 1))):
        part = pl.ds(start, size)
        layers += [
            pltpu.make_async_copy(u.at[:, part], to.at[pl.ds(0, 3)], arrived.at[3 * i]),
            pltpu.make_async_copy(v.at[:, part], to.at[pl.ds(3, 3)], arrived.at[3 * i + 1]),
            pltpu.make_async_copy(m.at[part], to.at[6], arrived.at[3 * i + 2]),
        ]
    for copy in layers:
        copy.start()
    for copy in first:
        copy.wait()
    live_count = counts[...]
    who = lax.broadcasted_iota(I32, (OWNERS, 128), 0)
    lane = lane_ids(1)
    hits = []
    for t in range(PAIRS // 128):
        live = lane + t * 128 < live_count
        target = jnp.where(live, owner[pl.ds(t, 1), :], -1)
        hits.append(jnp.where(who == target, 1.0, 0.0).astype(F32))
    before = jnp.where(
        lax.broadcasted_iota(I32, (128, 128), 0) < lax.broadcasted_iota(I32, (128, 128), 1), 1.0, 0.0
    ).astype(BF16)
    ranks = mm(jnp.concatenate([h.astype(BF16) for h in hits], axis=0), before)
    base = jnp.zeros((OWNERS, 1), F32)
    places = lax.broadcasted_iota(I32, (128, 128), 0)
    highs, lows, sides = [], [], []
    for t in range(PAIRS // 128):
        rank = jnp.sum(hits[t] * (ranks[t * OWNERS : (t + 1) * OWNERS] + base), axis=0, keepdims=True)
        base = base + jnp.sum(hits[t], axis=1, keepdims=True)
        here = places == rank.astype(I32)
        number = row[pl.ds(t, 1), :] + 1
        f = face[pl.ds(t, 1), :]
        f = f + jnp.where(f >= FACE_COLS, 1, 0) + jnp.where(f >= 2 * FACE_COLS, 1, 0) + 1
        highs.append(jnp.where(here, lax.shift_right_logical(number, 6).astype(F32), 0.0).astype(BF16))
        lows.append(jnp.where(here, (number & 63).astype(F32), 0.0).astype(BF16))
        sides.append(jnp.where(here, f.astype(F32), 0.0).astype(BF16))
    hit = jnp.concatenate([h.astype(BF16) for h in hits], axis=1)
    high = mm_nt(hit, jnp.concatenate(highs, axis=1))
    low = mm_nt(hit, jnp.concatenate(lows, axis=1))
    request[...] = (high * 64.0 + low).astype(I32)
    faces[...] = compact(mm_nt(hit, jnp.concatenate(sides, axis=1))).astype(I32)
    for copy in layers:
        copy.wait()


def side_kernel(u, v, m, z_low, z_high, y_up, y_down):
    for first, field, comps in ((0, u, 3), (3, v, 3), (6, m, 1)):
        for c in range(comps):
            n = first + c
            for out, h, y in ((y_up, 0, YN - 2), (y_up, 1, YN - 1), (y_down, 0, 0)):
                at = (n * (2 if out is y_up else 1) + h) * 24
                out[pl.ds(at, ZN), :] = field[pl.ds(c * ZN * YN + y, ZN, stride=YN), :]
                out[pl.ds(at + 16, 8), :] = jnp.zeros((8, 128), F32)
                out[pl.ds(at + 16, 1), :] = z_low[pl.ds((n * 2) * YN + y, 1), :]
                out[pl.ds(at + 17, 1), :] = z_low[pl.ds((n * 2 + 1) * YN + y, 1), :]
                out[pl.ds(at + 18, 1), :] = z_high[pl.ds(n * YN + y, 1), :]


def table_kernel(master, fixed, table):
    table[...] = mm3((fixed[:, 0:27], fixed[:, 128:155]), split(master[...]))


def stiffness_pair(stiffness, fixed):
    places = fixed[:, 512:593]
    high, low = split(stiffness[...])
    lower = (stiffness[...] - high.astype(F32) - low.astype(F32)).astype(BF16)
    spread = [mm_nt(mm(places, part).astype(BF16), places) for part in (high, low, lower)]
    high, low = split((spread[0] + spread[1]) + spread[2])
    return high + fixed[:, 0:144], low + fixed[:, 256:400]


def gather_kernel(ids, table, reply):
    numbers = jnp.maximum(compact(ids[...]) - 1, 0)
    found = []
    for c in range(CHUNKS):
        number = jnp.broadcast_to(numbers[c : c + 1], (8, 128))
        inside = number & 127
        outside = lax.shift_right_logical(number, 7)
        parts = []
        for f in range(4):
            total = pick_lanes(table[pl.ds(f * 8, 8), 0:128], inside)
            for k in range(1, ROWS // 128):
                piece = pick_lanes(table[pl.ds(f * 8, 8), k * 128 : (k + 1) * 128], inside)
                total = jnp.where(outside == k, piece, total)
            parts.append(total)
        found.append(parts)
    for c, tiles in enumerate(swap_groups(found)):
        for g in range(4):
            reply[g * CHUNKS + c] = tiles[g]


def slab(fields, halos, n, s):
    z_low, z_high, y_low, y_high = halos
    if s < 16:
        return fields[n // 3][pl.ds((n % 3 * ZN + s) * YN, YN), :]
    if s < 18:
        return z_low[pl.ds((n * 2 + s - 16) * YN, YN), :]
    if s < 19:
        return z_high[pl.ds(n * YN, YN), :]
    h, zb = divmod(s - 19, 3)
    if h < 2:
        return y_low[pl.ds((n * 2 + h) * 24 + zb * 8, 8), :]
    return y_high[pl.ds(n * 24 + zb * 8, 8), :]


def edge_kernel(u, v, m, z_low, z_high, y_low, y_high, reply_in, x_down, reply_out):
    fields, halos = (u, v, m), (z_low, z_high, y_low, y_high)
    lane = lane_ids(8)
    down = [jnp.zeros((8, 128), F32) for _ in range(2)]
    for c in range(4):
        for s in range(SLABS):
            k, spot = divmod(c * SLABS + s, 64)
            one = slab(fields, halos, 6 if c == 3 else c, s)
            two = one if c == 3 else slab(fields, halos, 3 + c, s)
            one = pltpu.roll(one, spot, 1) if spot else one
            two = pltpu.roll(two, 64 + spot, 1)
            down[k] = jnp.where(lane == spot, one, jnp.where(lane == 64 + spot, two, down[k]))
    for k in range(2):
        x_down[pl.ds(k * 8, 8), :] = down[k]


def element_kernel(
    edges, u, v, m, external, z_low, z_high, y_low, y_high, x_high, stiffness, fixed,
    residual, tangent, last, nodes, tiles_h, tiles_l, total,
):
    fields, halos = (u, v, m), (z_low, z_high, y_low, y_high)
    lane = lane_ids(8)
    low_half = lane < 64
    spot_of = lane & 63
    at_last = spot_of == 63
    even_even = 2 * spot_of
    odd_odd = 2 * spot_of + 1
    next_next = (2 * spot_of + 2) & 127

    def node_values(group):
        ones = [slab(fields, halos, 6 if c == 3 else c, s) for c, s in group]
        twos = [None if c == 3 else slab(fields, halos, 3 + c, s) for c, s in group]
        found = []
        for index in (even_even, odd_odd, next_next):
            first = [pick_lanes(one, index) for one in ones]
            second = [None if two is None else pick_lanes(two, index) for two in twos]
            found.append([a if b is None else jnp.where(low_half, a, b) for a, b in zip(first, second)])
        for i, (c, s) in enumerate(group):
            k, spot = divmod(c * SLABS + s, 64)
            held = x_high[pl.ds(k * 8, 8), :]
            after = held if spot == 63 else pltpu.roll(held, 63 - spot, 1)
            found[2][i] = jnp.where(at_last, after, found[2][i])
        return list(zip(*found))

    def put(value, s, at):
        if s < 19:
            z = s + 2 if s < 16 else (0, 1, 18)[s - 16]
            nodes[pl.ds(z * ZPITCH + 2 * YPITCH + at, 8, stride=YPITCH), :] = value
            return
        h, zb = divmod(s - 19, 3)
        base = (0, 1, 10)[h] * YPITCH + at
        if zb < 2:
            nodes[pl.ds((2 + zb * 8) * ZPITCH + base, 8, stride=ZPITCH), :] = value
        else:
            nodes[pl.ds(base, 1), :] = value[0:1]
            nodes[pl.ds(ZPITCH + base, 1), :] = value[1:2]
            nodes[pl.ds(18 * ZPITCH + base, 1), :] = value[2:3]

    todo = [(c, s) for c in range(4) for s in range(SLABS)]
    for start in range(0, len(todo), GROUP):
        group = todo[start : start + GROUP]
        values = node_values(group)
        for (c, s), three in zip(group, values):
            first, step = (9, 1) if c == 3 else (c, 3)
            for p in range(3):
                put(three[p], s, first + step * p)

    sub = lax.broadcasted_iota(I32, (TILE, 128), 0)
    one = jnp.where(sub == 12, 1.0, 0.0)

    def halve(z, carry):
        places = [pl.ds(pl.multiple_of(z * ZPITCH + y * YPITCH, TILE), TILE) for y in range(YE)]
        pairs = [split(jnp.where(sub < 12, nodes[at, :], one)) for at in places]
        for at, (high, low) in zip(places, pairs):
            tiles_h[at, :] = high
            tiles_l[at, :] = low
        return carry

    lax.fori_loop(0, ZE, halve, 0)

    x_last = jnp.where(edges[2] == lax.axis_size("gx") - 1, 63, 64)
    inside_x = jnp.where((lane_ids(1) & 63) < x_last, 1.0, 0.0)
    y_first = jnp.where(edges[1] == 0, 1, 0)
    y_last = jnp.where(edges[1] == lax.axis_size("gy") - 1, 3, 4)
    z_first = jnp.where(edges[0] == 0, 1, 0)
    z_last = jnp.where(edges[0] == lax.axis_size("gz") - 1, 7, 8)
    left_high, left_low = stiffness_pair(stiffness, fixed)

    total[pl.ds(0, ZPITCH), :] = jnp.zeros((ZPITCH, 128), F32)

    def inside_of(k, j):
        return (k >= z_first) & (k <= z_last) & (j >= y_first) & (j <= y_last)

    def products(elements):
        operands = []
        for tiles in (tiles_h, tiles_l):
            columns = []
            for k, j in elements:
                starts = [pl.multiple_of((2 * k + r) * ZPITCH + 2 * j * YPITCH, TILE) for r in range(3)]
                columns.append(jnp.concatenate([tiles[pl.ds(a, 3 * TILE), :] for a in starts], axis=0))
            operands.append(jnp.concatenate(columns, axis=1))
        both = mm3((left_high, left_low), operands)
        forces = []
        for i, (k, j) in enumerate(elements):
            mine = both[:, i * 128 : (i + 1) * 128]
            forces.append(mine * jnp.where(inside_of(k, j), mine[10:11] * inside_x, 0.0))
        return forces

    def part(force, r, q):
        return force[(3 * r + q) * TILE : (3 * r + q + 1) * TILE]

    def place_of(z, y):
        return pl.ds(pl.multiple_of(z * ZPITCH + y * YPITCH, TILE), TILE)

    def layers(i, carry):
        shared = None
        for j in range(5):
            one, two = products([(2 * i, j), (2 * i + 1, j)])
            for q in range(3):
                sums = [part(one, 0, q), part(one, 1, q), part(one, 2, q) + part(two, 0, q), part(two, 1, q), part(two, 2, q)]
                if q == 0 and shared is not None:
                    sums = [a + b for a, b in zip(sums, shared)]
                if q == 2 and j < 4:
                    shared = sums
                    continue
                y = 2 * j + q
                sums[0] = sums[0] + total[place_of(4 * i, y), :]
                for r in range(5):
                    total[place_of(4 * i + r, y), :] = sums[r]
        return carry

    lax.fori_loop(0, 4, layers, 0)
    last_layer = products([(8, 0), (8, 1)]) + products([(8, 2), (8, 3)]) + products([(8, 4)])
    for r in range(3):
        for y in range(YE):
            held = [part(last_layer[j], r, y - 2 * j) for j in range(5) if 0 <= y - 2 * j <= 2]
            held = held + [total[place_of(16, y), :]] if r == 0 else held
            total[place_of(16 + r, y), :] = sum(held[1:], held[0])

    half = lax.shift_right_logical(lane, 1)
    weave_u = half + jnp.where((lane & 1) == 0, 0, 64)
    weave_v = half + jnp.where((lane & 1) == 0, 64, 0)
    at_first = spot_of == 0
    sent = jnp.zeros((8, 128), F32)
    for start in range(0, ZN, 4):
        layer = range(start, start + 4)

        def rows(z, row):
            return total[pl.ds((z + 2) * ZPITCH + 2 * YPITCH + row, 8, stride=YPITCH), :]

        held = [rows(z, 9) for z in layer]
        p0 = [rows(z, c) for z in layer for c in range(3)]
        p1 = [rows(z, 3 + c) for z in layer for c in range(3)]
        p2 = [rows(z, 6 + c) for z in layer for c in range(3)]
        after = [pltpu.roll(x, 1, 1) for x in held + p2]
        odd = [pltpu.roll(x, 64, 1) for x in p1]
        for i, z in enumerate(layer):
            sent = jnp.where(spot_of == 48 + z, pltpu.roll(held[i], (z - 15) % 128, 1), sent)
            for c in range(3):
                moved = pltpu.roll(p2[3 * i + c], (c * 16 + z - 63) % 128, 1)
                sent = jnp.where(spot_of == c * 16 + z, moved, sent)
        after = [jnp.where(at_first, 0.0, x) for x in after]
        even = [a + b for a, b in zip(p0, after[4:])]
        mass = [pick_lanes(jnp.where(low_half, a + b, a), weave_u) for a, b in zip(held, after)]
        inner = [pick_lanes(jnp.where(low_half, a, b), weave_u) for a, b in zip(even, odd)]
        image = [pick_lanes(jnp.where(low_half, b, a), weave_v) for a, b in zip(even, odd)]
        results = []
        for i, z in enumerate(layer):
            for c in range(3):
                where = pl.ds((c * ZN + z) * YN, YN)
                uu, vv = u[where, :], v[where, :]
                square = uu * uu * mass[i]
                results.append(
                    (
                        where,
                        inner[3 * i + c] + 0.1 * square * uu - external[where, :],
                        image[3 * i + c] + 0.3 * square * vv,
                    )
                )
        for where, res, tan in results:
            residual[where, :] = res
            tangent[where, :] = tan
    last[...] = sent


def slot_kernel(u, v, faces, fixed, kin, selector, quads):
    plane = jnp.concatenate(
        [field[pl.ds(c * ZN * YN, YN), :] for field in (u, v) for c in range(3)], axis=0
    )
    wide = mm3(split(plane), (fixed[0:128, :], fixed[128:256, :]))
    tall = split(jnp.concatenate([wide[:, i * 128 : (i + 1) * 128] for i in range(6)], axis=0))
    for first, to in ((0, 0), (384, 128)):
        pair = fixed[256:312, first : first + 288], fixed[320:376, first : first + 288]
        quads[:, to : to + 128] = mm3(pair, tall)
    slot_faces = faces[...]
    face_ids = lax.broadcasted_iota(I32, (FACES, 128), 0) + 1
    for c in range(CHUNKS):
        slot_face = slot_faces[c : c + 1]
        index = jnp.maximum(jnp.broadcast_to(slot_face, (8, 128)) - 1, 0)
        inside, outside = index & 127, index >= 128
        for i in range(7):
            kin[c, pl.ds(i * 8, 8), :] = jnp.where(
                outside,
                pick_lanes(quads[pl.ds(i * 8, 8), 128:256], inside),
                pick_lanes(quads[pl.ds(i * 8, 8), 0:128], inside),
            )
        selector[:, c * 128 : (c + 1) * 128] = jnp.where(face_ids == slot_face, 1.0, 0.0).astype(BF16)


def contact_kernel(replies, kin, selector, fixed, left, u, v, res_in, tan_in, residual, tangent):
    values_h, values_l = [], []
    records = swap_groups([[replies[g * CHUNKS + c] for g in range(4)] for c in range(CHUNKS)])
    for c in range(CHUNKS):
        m = records[c]

        def point(m0, m1, m2, k):
            gap = m0 + m1 * k[0] + m2 * k[1] + k[2]
            scaled = -2.0 * gap
            small = jnp.exp(-jnp.abs(scaled))
            pressure = 2.0 * (jnp.maximum(scaled, 0.0) + jnp.log1p(small))
            slope = 4.0 * jnp.where(scaled >= 0.0, 1.0, small) / (1.0 + small)
            push = slope * (m1 * k[3] + m2 * k[4] + k[5])
            return pressure * m1, pressure * m2, pressure, push * m1, push * m2, push

        main = point(m[0], m[1], m[2], [kin[c, pl.ds(i * 8, 8), :] for i in range(6)])
        ends = kin[c, pl.ds(48, 8), :]
        ninth = point(m[3][0:1], m[3][1:2], m[3][2:3], [ends[i : i + 1] for i in range(6)])
        stack = jnp.concatenate(list(main) + list(ninth) + [jnp.zeros((10, 128), F32)], axis=0)
        high, low = split(stack)
        values_h.append(high)
        values_l.append(low)
    values = jnp.concatenate(
        [jnp.concatenate(values_h, axis=1), jnp.concatenate(values_l, axis=1)], axis=0
    )
    sums = mm_nt(values, selector[...])
    sums = sums[0:64] + sums[64:128]
    sums = jnp.concatenate([sums[:, 0:64], sums[:, 64:128], sums[:, 128:192]], axis=0)
    along = mm3(split(sums), (fixed[0:64, 0:384], fixed[64:128, 0:384]))
    tall = split(jnp.concatenate([along[:, i * 128 : (i + 1) * 128] for i in range(3)], axis=0))
    plane = mm3((fixed[128:176, :], fixed[176:224, :]), tall)
    at_first = lane_ids(8) == 0
    came = left[...]
    for z in range(ZN):
        mass = pltpu.roll(came, 80 - z, 1)
        for c in range(3):
            where = pl.ds((c * ZN + z) * YN, YN)
            uu, vv = u[where, :], v[where, :]
            square = uu * uu * mass
            spot = c * 16 + z
            inner = came if spot == 0 else pltpu.roll(came, 128 - spot, 1)
            image = pltpu.roll(came, 64 - spot, 1)
            res = res_in[where, :] + jnp.where(at_first, inner + 0.1 * square * uu, 0.0)
            tan = tan_in[where, :] + jnp.where(at_first, image + 0.3 * square * vv, 0.0)
            if z == 0:
                res = res + plane[c * 8 : c * 8 + 8]
                tan = tan + plane[24 + c * 8 : 32 + c * 8]
            residual[where, :] = res
            tangent[where, :] = tan


def call(body, outs, scratch=(), smem=(), free=(), hbm=(), free_out=(), flops=0, n=0, limit=45056, **more):
    places = [
        pltpu.SMEM if i in smem else pl.ANY if i in free else pltpu.HBM if i in hbm else pltpu.VMEM
        for i in range(n)
    ]
    specs = [pl.BlockSpec(memory_space=place) for place in places]
    return pl.pallas_call(
        body,
        out_shape=tuple(jax.ShapeDtypeStruct(s, t) for s, t in outs),
        in_specs=specs,
        out_specs=tuple(
            pl.BlockSpec(memory_space=pl.ANY if i in free_out else pltpu.VMEM) for i in range(len(outs))
        ),
        scratch_shapes=list(scratch),
        cost_estimate=pl.CostEstimate(flops=flops, bytes_accessed=0, transcendentals=0),
        compiler_params=pltpu.CompilerParams(vmem_limit_bytes=limit << 10),
        **more,
    )


def ring(values, axis, up):
    count = lax.axis_size(axis)
    pairs = [(i, (i + 1) % count) if up else ((i + 1) % count, i) for i in range(count)]
    return lax.ppermute(values, axis, pairs)


def local(
    displacement,
    direction,
    modulus,
    external,
    stiffness,
    master_record,
    pair_face,
    pair_owner,
    pair_row,
    pair_count,
):
    u = displacement.reshape(3 * ZN * YN, XN)
    v = direction.reshape(3 * ZN * YN, XN)
    m = modulus.reshape(ZN * YN, XN)
    request, faces, z_up, z_down = call(
        request_kernel,
        [((OWNERS, 128), I32), ((CHUNKS, 128), I32), ((7, 2, YN, XN), F32), ((7, 1, YN, XN), F32)],
        scratch=[
            pltpu.VMEM((8, 128), I32), pltpu.VMEM((8, 128), I32), pltpu.VMEM((8, 128), I32),
            pltpu.SemaphoreType.DMA((9,)),
        ],
        hbm=(0, 1, 2, 4, 5, 6), n=7, limit=64512,
    )(
        pair_owner.reshape(8, 128), pair_row.reshape(8, 128), pair_face.reshape(8, 128), pair_count,
        displacement, direction, modulus,
    )
    z_low = ring(z_up, "gz", True).reshape(7 * 2 * YN, XN)
    z_high = ring(z_down, "gz", False).reshape(7 * YN, XN)
    ids = lax.all_to_all(request, GROUPS, split_axis=0, concat_axis=0, tiled=True)

    (table,) = call(table_kernel, [((32, ROWS), F32)], n=2)(master_record, jnp.asarray(table_constants()))
    kin, selector = call(
        slot_kernel, [((CHUNKS, 56, 128), F32), ((FACES, OWNERS * CAP), BF16)],
        scratch=[pltpu.VMEM((56, 256), F32)], n=4,
    )(u, v, faces, jnp.asarray(slot_constants()))
    y_up, y_down = call(side_kernel, [((7 * 2 * 24, XN), F32), ((7 * 24, XN), F32)], n=5)(
        u, v, m, z_low, z_high
    )
    y_low = ring(y_up, "gy", True)
    y_high = ring(y_down, "gy", False)

    (reply,) = call(gather_kernel, [((OWNERS, 8, 128), F32)], n=2, flops=5 << 28)(ids, table)
    x_down, reply = call(
        edge_kernel, [((16, 128), F32), ((OWNERS, 8, 128), F32)], n=8, free=(7,), free_out=(1,),
        input_output_aliases={7: 1},
    )(u, v, m, z_low, z_high, y_low, y_high, reply)
    x_high = ring(x_down, "gx", False)
    replies = lax.all_to_all(reply, GROUPS, split_axis=0, concat_axis=0, tiled=True)

    edges = jnp.stack([lax.axis_index(a).astype(I32) for a in ("gz", "gy", "gx")])
    residual, tangent, last = call(
        element_kernel,
        [((3 * ZN * YN, XN), F32), ((3 * ZN * YN, XN), F32), ((8, 128), F32)],
        scratch=[
            pltpu.VMEM((NODE_ROWS, 128), F32),
            pltpu.VMEM((NODE_ROWS, 128), BF16),
            pltpu.VMEM((NODE_ROWS, 128), BF16),
            pltpu.VMEM((NODE_ROWS, 128), F32),
        ],
        smem=(0,), n=12, flops=1 << 33,
    )(
        edges, u, v, m, external.reshape(3 * ZN * YN, XN), z_low, z_high, y_low, y_high, x_high,
        stiffness, jnp.asarray(element_constants()),
    )
    left = ring(last, "gx", True)
    residual, tangent = call(
        contact_kernel, [((3 * ZN * YN, XN), F32), ((3 * ZN * YN, XN), F32)], n=9, flops=1 << 20
    )(replies, kin, selector, jnp.asarray(contact_constants()), left, u, v, residual, tangent)
    return residual.reshape(3, ZN, YN, XN), tangent.reshape(3, ZN, YN, XN)


def solution(mesh):
    placed = (
        P(None, "gz", "gy", "gx"),
        P(None, "gz", "gy", "gx"),
        P("gz", "gy", "gx"),
        P(None, "gz", "gy", "gx"),
        P(),
        P(None, ("gx", "gy", "gz")),
        P(("gx", "gy", "gz")),
        P(("gx", "gy", "gz"), None),
        P(("gx", "gy", "gz")),
        P(("gx", "gy", "gz")),
    )
    return jax.shard_map(
        local,
        mesh=mesh,
        in_specs=placed,
        out_specs=(P(None, "gz", "gy", "gx"), P(None, "gz", "gy", "gx")),
        check_vma=False,
    )
```

```python
import jax
import jax.numpy as jnp
import numpy as np
from jax import lax
from jax.experimental import pallas as pl
from jax.experimental.pallas import tpu as pltpu
from jax.sharding import PartitionSpec as P

F32 = jnp.float32
BF16 = jnp.bfloat16
I32 = jnp.int32

ZN, YN, XN = 16, 8, 128
ZE, YE = ZN + 3, YN + 3
OWNERS, CAP, PAIRS, ROWS = 64, 32, 1024, 2048
CHUNKS = OWNERS * CAP // 128
FACE_ROWS, FACE_COLS, FACE_LANES = 3, 63, 64
FACES = FACE_ROWS * FACE_LANES
SLABS = 28
TILE = 16
YPITCH = TILE
ZPITCH = YE * TILE
NODE_ROWS = ZE * ZPITCH
BLOCK = 9 * TILE
GROUPS = ("gx", "gy")
GROUP = 14


def shapes_1d():
    points = np.array([-np.sqrt(0.6), 0.0, np.sqrt(0.6)])
    gauss = np.array([5.0, 8.0, 5.0]) / 9.0
    line = np.stack(
        [points * (points - 1.0) / 2.0, 1.0 - points * points, points * (points + 1.0) / 2.0],
        axis=1,
    )
    return line, gauss


def halves(values):
    high = np.asarray(values, np.float32).astype(jnp.bfloat16)
    low = (np.asarray(values, np.float64) - high.astype(np.float64)).astype(jnp.bfloat16)
    return high, low


def record_map():
    line, _ = shapes_1d()
    out = np.zeros((32, 27))
    for k in range(3):
        for qy in range(3):
            for qx in range(3):
                q = 3 * qy + qx
                row = k * 8 + q if q < 8 else 24 + k
                for b in range(3):
                    for a in range(3):
                        out[row, 9 * k + 3 * b + a] = line[qy, b] * line[qx, a]
    return halves(out)


def quad_row(part, q):
    return part * 8 + q if q < 8 else 48 + part


def face_x_map():
    line, _ = shapes_1d()
    out = np.zeros((128, 6 * 128))
    for qx in range(3):
        for side in range(2):
            for fx in range(FACE_COLS):
                for a in range(3):
                    out[2 * fx + a, (2 * qx + side) * 128 + side * 64 + fx] = line[qx, a]
    return halves(out)


def face_y_map():
    line, _ = shapes_1d()
    first = np.zeros((56, 6 * 48))
    second = np.zeros((56, 6 * 48))
    for part in range(6):
        for qy in range(3):
            for qx in range(3):
                row = quad_row(part, 3 * qy + qx)
                for b in range(3):
                    first[row, (2 * qx) * 48 + part * 8 + b] = line[qy, b]
                    first[row, (2 * qx + 1) * 48 + part * 8 + 2 + b] = line[qy, b]
                    second[row, (2 * qx) * 48 + part * 8 + 4 + b] = line[qy, b]
    return halves(first), halves(second)


def node_x_map():
    line, _ = shapes_1d()
    out = np.zeros((FACE_LANES, 3 * 128))
    for qx in range(3):
        for fx in range(FACE_COLS):
            for a in range(3):
                out[fx, qx * 128 + 2 * fx + a] = line[qx, a]
    return halves(out)


def node_y_map():
    line, gauss = shapes_1d()
    out = np.zeros((48, 3 * FACE_ROWS * 64))
    for part in range(6):
        for qx in range(3):
            for qy in range(3):
                weight = 0.25 * gauss[qx] * gauss[qy] * (-1.0 if part < 3 else 1.0)
                for fy in range(FACE_ROWS):
                    for b in range(3):
                        column = qx * FACE_ROWS * 64 + fy * 64 + quad_row(part, 3 * qy + qx)
                        out[part * 8 + 2 * fy + b, column] = weight * line[qy, b]
    return halves(out)


def stiffness_places():
    place = np.zeros((BLOCK, 81))
    for block in range(9):
        for p in range(3):
            for c in range(3):
                place[block * TILE + 3 * p + c, block * 9 + 3 * p + c] = 1.0
    fixed = np.zeros((BLOCK, BLOCK))
    for block in range(9):
        fixed[block * TILE + 9, block * TILE + 12] = 1.0
        for p in range(3):
            fixed[10, block * TILE + 9 + p] = 1.0 / 27.0
    fixed[[b * TILE + 9 for b in range(1, 9)], :] = 0.0
    for block in range(1, 9):
        fixed[block * TILE + 9, block * TILE + 12] = 1.0
    return place.astype(np.float32), halves(fixed)


def packed(pieces, rows, columns):
    out = np.zeros((rows, columns), jnp.bfloat16)
    for row, column, piece in pieces:
        out[row : row + piece.shape[0], column : column + piece.shape[1]] = piece
    return out


def element_constants():
    place, fixed = stiffness_places()
    return packed([(0, 0, fixed[0]), (0, 256, fixed[1]), (0, 512, place.astype(jnp.bfloat16))], 144, 640)


def slot_constants():
    along = face_x_map()
    first, second = face_y_map()
    pieces = [
        (0, 0, along[0]), (128, 0, along[1]),
        (256, 0, first[0]), (256, 384, second[0]), (320, 0, first[1]), (320, 384, second[1]),
    ]
    return packed(pieces, 384, 768)


def table_constants():
    high, low = record_map()
    return packed([(0, 0, high), (0, 128, low)], 32, 256)


def contact_constants():
    along, across = node_x_map(), node_y_map()
    pieces = [(0, 0, along[0]), (64, 0, along[1]), (128, 0, across[0]), (176, 0, across[1])]
    return packed(pieces, 224, 576)


def split(values):
    high = values.astype(BF16)
    return high, (values - high.astype(F32)).astype(BF16)


def mm(a, b):
    return jnp.dot(a, b, preferred_element_type=F32)


def mm_nt(a, b):
    return lax.dot_general(a, b, (((1,), (1,)), ((), ())), preferred_element_type=F32)


def mm3(a, b):
    return mm(a[0], b[0]) + (mm(a[0], b[1]) + mm(a[1], b[0]))


def lane_ids(rows):
    return lax.broadcasted_iota(I32, (rows, 128), 1)


def pick_lanes(values, index):
    return jnp.take_along_axis(values, index, axis=1, mode="promise_in_bounds")


def compact(values):
    return (
        values[0:16]
        + pltpu.roll(values[16:32], 32, 1)
        + pltpu.roll(values[32:48], 64, 1)
        + pltpu.roll(values[48:64], 96, 1)
    )


def by_group(lane, parts):
    odd = (lane & 32) != 0
    return jnp.where(lane < 64, jnp.where(odd, parts[1], parts[0]), jnp.where(odd, parts[3], parts[2]))


def swap_groups(quads):
    lane = lane_ids(8)
    moved = [[by_group(lane, [q[(g + r) % 4] for g in range(4)]) for q in quads] for r in range(4)]
    for r in range(1, 4):
        moved[r] = [pltpu.roll(x, 32 * r, 1) for x in moved[r]]
    return [
        [by_group(lane, [moved[(f - g) % 4][i] for f in range(4)]) for g in range(4)]
        for i in range(len(quads))
    ]


def request_kernel(
    owners, rows, sides_in, u, v, m, request, codes, z_up, z_down, owner, row, face, arrived
):
    first = [
        pltpu.make_async_copy(source, to, arrived.at[6 + i])
        for i, (source, to) in enumerate(((owners, owner), (rows, row), (sides_in, face)))
    ]
    for copy in first:
        copy.start()
    layers = []
    for i, (to, start, size) in enumerate(((z_up, ZN - 2, 2), (z_down, 0, 1))):
        part = pl.ds(start, size)
        layers += [
            pltpu.make_async_copy(u.at[:, part], to.at[pl.ds(0, 3)], arrived.at[3 * i]),
            pltpu.make_async_copy(v.at[:, part], to.at[pl.ds(3, 3)], arrived.at[3 * i + 1]),
            pltpu.make_async_copy(m.at[part], to.at[6], arrived.at[3 * i + 2]),
        ]
    for copy in layers:
        copy.start()
    for copy in first:
        copy.wait()
    who = lax.broadcasted_iota(I32, (OWNERS, 128), 0)
    lane = lane_ids(1)
    hits = []
    for t in range(PAIRS // 128):
        hits.append(jnp.where(who == owner[pl.ds(t, 1), :], 1.0, 0.0).astype(F32))
    before = jnp.where(
        lax.broadcasted_iota(I32, (128, 128), 0) < lax.broadcasted_iota(I32, (128, 128), 1), 1.0, 0.0
    ).astype(BF16)
    ranks = mm(jnp.concatenate([h.astype(BF16) for h in hits], axis=0), before)
    base = jnp.zeros((OWNERS, 1), F32)
    places = lax.broadcasted_iota(I32, (128, 128), 0)
    highs, lows, sides, marks = [], [], [], []
    for t in range(PAIRS // 128):
        rank = jnp.sum(hits[t] * (ranks[t * OWNERS : (t + 1) * OWNERS] + base), axis=0, keepdims=True)
        base = base + jnp.sum(hits[t], axis=1, keepdims=True)
        here = places == rank.astype(I32)
        number = row[pl.ds(t, 1), :] + 1
        f = face[pl.ds(t, 1), :]
        f = f + jnp.where(f >= FACE_COLS, 1, 0) + jnp.where(f >= 2 * FACE_COLS, 1, 0) + 1
        spot = lane + t * 128
        numbers = (
            lax.shift_right_logical(number, 6) + 64 * (t // 2),
            (number & 63) + 64 * (lax.shift_right_logical(spot, 6) & 3),
            f,
            spot & 63,
        )
        for to, value in zip((highs, lows, sides, marks), numbers):
            to.append(jnp.where(here, value.astype(F32), 0.0).astype(BF16))
    hit = jnp.concatenate([h.astype(BF16) for h in hits], axis=1)
    high, low, side, mark = (
        mm_nt(hit, jnp.concatenate(to, axis=1)).astype(I32) for to in (highs, lows, sides, marks)
    )
    request[...] = (high & 63) * 64 + (low & 63)
    spots = lax.shift_right_logical(high, 6) * 256 + lax.shift_right_logical(low, 6) * 64 + mark
    codes[...] = compact(spots * 256 + side)
    for copy in layers:
        copy.wait()


def side_kernel(u, v, m, z_low, z_high, y_up, y_down):
    for first, field, comps in ((0, u, 3), (3, v, 3), (6, m, 1)):
        for c in range(comps):
            n = first + c
            for out, h, y in ((y_up, 0, YN - 2), (y_up, 1, YN - 1), (y_down, 0, 0)):
                at = (n * (2 if out is y_up else 1) + h) * 24
                out[pl.ds(at, ZN), :] = field[pl.ds(c * ZN * YN + y, ZN, stride=YN), :]
                out[pl.ds(at + 16, 8), :] = jnp.zeros((8, 128), F32)
                out[pl.ds(at + 16, 1), :] = z_low[pl.ds((n * 2) * YN + y, 1), :]
                out[pl.ds(at + 17, 1), :] = z_low[pl.ds((n * 2 + 1) * YN + y, 1), :]
                out[pl.ds(at + 18, 1), :] = z_high[pl.ds(n * YN + y, 1), :]


def table_kernel(master, fixed, table):
    table[...] = mm3((fixed[:, 0:27], fixed[:, 128:155]), split(master[...]))


def stiffness_pair(stiffness, fixed):
    places = fixed[:, 512:593]
    high, low = split(stiffness[...])
    lower = (stiffness[...] - high.astype(F32) - low.astype(F32)).astype(BF16)
    spread = [mm_nt(mm(places, part).astype(BF16), places) for part in (high, low, lower)]
    high, low = split((spread[0] + spread[1]) + spread[2])
    return high + fixed[:, 0:144], low + fixed[:, 256:400]


def gather_kernel(ids, table, reply):
    numbers = jnp.maximum(compact(ids[...]) - 1, 0)
    found = []
    for c in range(CHUNKS):
        number = jnp.broadcast_to(numbers[c : c + 1], (8, 128))
        inside = number & 127
        outside = lax.shift_right_logical(number, 7)
        parts = []
        for f in range(4):
            total = pick_lanes(table[pl.ds(f * 8, 8), 0:128], inside)
            for k in range(1, ROWS // 128):
                piece = pick_lanes(table[pl.ds(f * 8, 8), k * 128 : (k + 1) * 128], inside)
                total = jnp.where(outside == k, piece, total)
            parts.append(total)
        found.append(parts)
    for c, tiles in enumerate(swap_groups(found)):
        for g in range(4):
            reply[g * CHUNKS + c] = tiles[g]


def slab(fields, halos, n, s):
    z_low, z_high, y_low, y_high = halos
    if s < 16:
        return fields[n // 3][pl.ds((n % 3 * ZN + s) * YN, YN), :]
    if s < 18:
        return z_low[pl.ds((n * 2 + s - 16) * YN, YN), :]
    if s < 19:
        return z_high[pl.ds(n * YN, YN), :]
    h, zb = divmod(s - 19, 3)
    if h < 2:
        return y_low[pl.ds((n * 2 + h) * 24 + zb * 8, 8), :]
    return y_high[pl.ds(n * 24 + zb * 8, 8), :]


def edge_kernel(u, v, m, z_low, z_high, y_low, y_high, reply_in, x_down, reply_out):
    fields, halos = (u, v, m), (z_low, z_high, y_low, y_high)
    lane = lane_ids(8)
    down = [jnp.zeros((8, 128), F32) for _ in range(2)]
    for c in range(4):
        for s in range(SLABS):
            k, spot = divmod(c * SLABS + s, 64)
            one = slab(fields, halos, 6 if c == 3 else c, s)
            two = one if c == 3 else slab(fields, halos, 3 + c, s)
            one = pltpu.roll(one, spot, 1) if spot else one
            two = pltpu.roll(two, 64 + spot, 1)
            down[k] = jnp.where(lane == spot, one, jnp.where(lane == 64 + spot, two, down[k]))
    for k in range(2):
        x_down[pl.ds(k * 8, 8), :] = down[k]


def element_kernel(
    edges, u, v, m, external, z_low, z_high, y_low, y_high, x_high, stiffness, fixed,
    residual, tangent, last, nodes, tiles_h, tiles_l, total,
):
    fields, halos = (u, v, m), (z_low, z_high, y_low, y_high)
    lane = lane_ids(8)
    low_half = lane < 64
    spot_of = lane & 63
    at_last = spot_of == 63
    even_even = 2 * spot_of
    odd_odd = 2 * spot_of + 1
    next_next = (2 * spot_of + 2) & 127

    def node_values(group):
        ones = [slab(fields, halos, 6 if c == 3 else c, s) for c, s in group]
        twos = [None if c == 3 else slab(fields, halos, 3 + c, s) for c, s in group]
        found = []
        for index in (even_even, odd_odd, next_next):
            first = [pick_lanes(one, index) for one in ones]
            second = [None if two is None else pick_lanes(two, index) for two in twos]
            found.append([a if b is None else jnp.where(low_half, a, b) for a, b in zip(first, second)])
        for i, (c, s) in enumerate(group):
            k, spot = divmod(c * SLABS + s, 64)
            held = x_high[pl.ds(k * 8, 8), :]
            after = held if spot == 63 else pltpu.roll(held, 63 - spot, 1)
            found[2][i] = jnp.where(at_last, after, found[2][i])
        return list(zip(*found))

    def put(value, s, at):
        if s < 19:
            z = s + 2 if s < 16 else (0, 1, 18)[s - 16]
            nodes[pl.ds(z * ZPITCH + 2 * YPITCH + at, 8, stride=YPITCH), :] = value
            return
        h, zb = divmod(s - 19, 3)
        base = (0, 1, 10)[h] * YPITCH + at
        if zb < 2:
            nodes[pl.ds((2 + zb * 8) * ZPITCH + base, 8, stride=ZPITCH), :] = value
        else:
            nodes[pl.ds(base, 1), :] = value[0:1]
            nodes[pl.ds(ZPITCH + base, 1), :] = value[1:2]
            nodes[pl.ds(18 * ZPITCH + base, 1), :] = value[2:3]

    todo = [(c, s) for c in range(4) for s in range(SLABS)]
    for start in range(0, len(todo), GROUP):
        group = todo[start : start + GROUP]
        values = node_values(group)
        for (c, s), three in zip(group, values):
            first, step = (9, 1) if c == 3 else (c, 3)
            for p in range(3):
                put(three[p], s, first + step * p)

    sub = lax.broadcasted_iota(I32, (TILE, 128), 0)
    one = jnp.where(sub == 12, 1.0, 0.0)

    def halve(z, carry):
        places = [pl.ds(pl.multiple_of(z * ZPITCH + y * YPITCH, TILE), TILE) for y in range(YE)]
        pairs = [split(jnp.where(sub < 12, nodes[at, :], one)) for at in places]
        for at, (high, low) in zip(places, pairs):
            tiles_h[at, :] = high
            tiles_l[at, :] = low
        return carry

    lax.fori_loop(0, ZE, halve, 0)

    x_last = jnp.where(edges[2] == lax.axis_size("gx") - 1, 63, 64)
    inside_x = jnp.where((lane_ids(1) & 63) < x_last, 1.0, 0.0)
    y_first = jnp.where(edges[1] == 0, 1, 0)
    y_last = jnp.where(edges[1] == lax.axis_size("gy") - 1, 3, 4)
    z_first = jnp.where(edges[0] == 0, 1, 0)
    z_last = jnp.where(edges[0] == lax.axis_size("gz") - 1, 7, 8)
    left_high, left_low = stiffness_pair(stiffness, fixed)

    total[pl.ds(0, ZPITCH), :] = jnp.zeros((ZPITCH, 128), F32)

    def inside_of(k, j):
        return (k >= z_first) & (k <= z_last) & (j >= y_first) & (j <= y_last)

    def products(elements):
        operands = []
        for tiles in (tiles_h, tiles_l):
            columns = []
            for k, j in elements:
                starts = [pl.multiple_of((2 * k + r) * ZPITCH + 2 * j * YPITCH, TILE) for r in range(3)]
                columns.append(jnp.concatenate([tiles[pl.ds(a, 3 * TILE), :] for a in starts], axis=0))
            operands.append(jnp.concatenate(columns, axis=1))
        both = mm3((left_high, left_low), operands)
        forces = []
        for i, (k, j) in enumerate(elements):
            mine = both[:, i * 128 : (i + 1) * 128]
            forces.append(mine * jnp.where(inside_of(k, j), mine[10:11] * inside_x, 0.0))
        return forces

    def part(force, r, q):
        return force[(3 * r + q) * TILE : (3 * r + q + 1) * TILE]

    def place_of(z, y):
        return pl.ds(pl.multiple_of(z * ZPITCH + y * YPITCH, TILE), TILE)

    def layers(i, carry):
        shared = None
        for j in range(5):
            one, two = products([(2 * i, j), (2 * i + 1, j)])
            for q in range(3):
                sums = [part(one, 0, q), part(one, 1, q), part(one, 2, q) + part(two, 0, q), part(two, 1, q), part(two, 2, q)]
                if q == 0 and shared is not None:
                    sums = [a + b for a, b in zip(sums, shared)]
                if q == 2 and j < 4:
                    shared = sums
                    continue
                y = 2 * j + q
                sums[0] = sums[0] + total[place_of(4 * i, y), :]
                for r in range(5):
                    total[place_of(4 * i + r, y), :] = sums[r]
        return carry

    lax.fori_loop(0, 4, layers, 0)
    last_layer = products([(8, 0), (8, 1)]) + products([(8, 2), (8, 3)]) + products([(8, 4)])
    for r in range(3):
        for y in range(YE):
            held = [part(last_layer[j], r, y - 2 * j) for j in range(5) if 0 <= y - 2 * j <= 2]
            held = held + [total[place_of(16, y), :]] if r == 0 else held
            total[place_of(16 + r, y), :] = sum(held[1:], held[0])

    half = lax.shift_right_logical(lane, 1)
    weave_u = half + jnp.where((lane & 1) == 0, 0, 64)
    weave_v = half + jnp.where((lane & 1) == 0, 64, 0)
    at_first = spot_of == 0
    sent = jnp.zeros((8, 128), F32)
    for start in range(0, ZN, 4):
        layer = range(start, start + 4)

        def rows(z, row):
            return total[pl.ds((z + 2) * ZPITCH + 2 * YPITCH + row, 8, stride=YPITCH), :]

        held = [rows(z, 9) for z in layer]
        p0 = [rows(z, c) for z in layer for c in range(3)]
        p1 = [rows(z, 3 + c) for z in layer for c in range(3)]
        p2 = [rows(z, 6 + c) for z in layer for c in range(3)]
        after = [pltpu.roll(x, 1, 1) for x in held + p2]
        odd = [pltpu.roll(x, 64, 1) for x in p1]
        for i, z in enumerate(layer):
            sent = jnp.where(spot_of == 48 + z, pltpu.roll(held[i], (z - 15) % 128, 1), sent)
            for c in range(3):
                moved = pltpu.roll(p2[3 * i + c], (c * 16 + z - 63) % 128, 1)
                sent = jnp.where(spot_of == c * 16 + z, moved, sent)
        after = [jnp.where(at_first, 0.0, x) for x in after]
        even = [a + b for a, b in zip(p0, after[4:])]
        mass = [pick_lanes(jnp.where(low_half, a + b, a), weave_u) for a, b in zip(held, after)]
        inner = [pick_lanes(jnp.where(low_half, a, b), weave_u) for a, b in zip(even, odd)]
        image = [pick_lanes(jnp.where(low_half, b, a), weave_v) for a, b in zip(even, odd)]
        results = []
        for i, z in enumerate(layer):
            for c in range(3):
                where = pl.ds((c * ZN + z) * YN, YN)
                uu, vv = u[where, :], v[where, :]
                square = uu * uu * mass[i]
                results.append(
                    (
                        where,
                        inner[3 * i + c] + 0.1 * square * uu - external[where, :],
                        image[3 * i + c] + 0.3 * square * vv,
                    )
                )
        for where, res, tan in results:
            residual[where, :] = res
            tangent[where, :] = tan
    last[...] = sent


def slot_kernel(u, v, codes, fixed, count, kin, selector, quads):
    plane = jnp.concatenate(
        [field[pl.ds(c * ZN * YN, YN), :] for field in (u, v) for c in range(3)], axis=0
    )
    wide = mm3(split(plane), (fixed[0:128, :], fixed[128:256, :]))
    tall = split(jnp.concatenate([wide[:, i * 128 : (i + 1) * 128] for i in range(6)], axis=0))
    for first, to in ((0, 0), (384, 128)):
        pair = fixed[256:312, first : first + 288], fixed[320:376, first : first + 288]
        quads[:, to : to + 128] = mm3(pair, tall)
    spots = lax.shift_right_logical(codes[...], 8)
    slot_faces = jnp.where(spots < count[0], codes[...] & 255, 0)
    columns = jnp.concatenate([slot_faces.astype(F32), jnp.zeros((112, 128), F32)], axis=0).T
    face_ids = (lax.broadcasted_iota(I32, (128, FACES), 1) + 1).astype(F32)
    for c in range(CHUNKS):
        slot_face = slot_faces[c : c + 1]
        index = jnp.maximum(jnp.broadcast_to(slot_face, (8, 128)) - 1, 0)
        inside, outside = index & 127, index >= 128
        for i in range(7):
            kin[c, pl.ds(i * 8, 8), :] = jnp.where(
                outside,
                pick_lanes(quads[pl.ds(i * 8, 8), 128:256], inside),
                pick_lanes(quads[pl.ds(i * 8, 8), 0:128], inside),
            )
        selector[pl.ds(c * 128, 128), :] = jnp.where(face_ids == columns[:, c : c + 1], 1.0, 0.0).astype(BF16)


def contact_kernel(replies, kin, selector, fixed, left, u, v, res_in, tan_in, residual, tangent):
    values_h, values_l = [], []
    records = swap_groups([[replies[g * CHUNKS + c] for g in range(4)] for c in range(CHUNKS)])
    for c in range(CHUNKS):
        m = records[c]

        def point(m0, m1, m2, k):
            gap = m0 + m1 * k[0] + m2 * k[1] + k[2]
            scaled = -2.0 * gap
            small = jnp.exp(-jnp.abs(scaled))
            pressure = 2.0 * (jnp.maximum(scaled, 0.0) + jnp.log1p(small))
            slope = 4.0 * jnp.where(scaled >= 0.0, 1.0, small) / (1.0 + small)
            push = slope * (m1 * k[3] + m2 * k[4] + k[5])
            return pressure * m1, pressure * m2, pressure, push * m1, push * m2, push

        main = point(m[0], m[1], m[2], [kin[c, pl.ds(i * 8, 8), :] for i in range(6)])
        ends = kin[c, pl.ds(48, 8), :]
        ninth = point(m[3][0:1], m[3][1:2], m[3][2:3], [ends[i : i + 1] for i in range(6)])
        stack = jnp.concatenate(list(main) + list(ninth) + [jnp.zeros((10, 128), F32)], axis=0)
        high, low = split(stack)
        values_h.append(high)
        values_l.append(low)
    values = jnp.concatenate(
        [jnp.concatenate(values_h, axis=1), jnp.concatenate(values_l, axis=1)], axis=0
    )
    sums = mm(values, selector[...])
    sums = sums[0:64] + sums[64:128]
    sums = jnp.concatenate([sums[:, 0:64], sums[:, 64:128], sums[:, 128:192]], axis=0)
    along = mm3(split(sums), (fixed[0:64, 0:384], fixed[64:128, 0:384]))
    tall = split(jnp.concatenate([along[:, i * 128 : (i + 1) * 128] for i in range(3)], axis=0))
    plane = mm3((fixed[128:176, :], fixed[176:224, :]), tall)
    at_first = lane_ids(8) == 0
    came = left[...]
    for z in range(ZN):
        mass = pltpu.roll(came, 80 - z, 1)
        for c in range(3):
            where = pl.ds((c * ZN + z) * YN, YN)
            uu, vv = u[where, :], v[where, :]
            square = uu * uu * mass
            spot = c * 16 + z
            inner = came if spot == 0 else pltpu.roll(came, 128 - spot, 1)
            image = pltpu.roll(came, 64 - spot, 1)
            res = res_in[where, :] + jnp.where(at_first, inner + 0.1 * square * uu, 0.0)
            tan = tan_in[where, :] + jnp.where(at_first, image + 0.3 * square * vv, 0.0)
            if z == 0:
                res = res + plane[c * 8 : c * 8 + 8]
                tan = tan + plane[24 + c * 8 : 32 + c * 8]
            residual[where, :] = res
            tangent[where, :] = tan


def call(body, outs, scratch=(), smem=(), free=(), hbm=(), free_out=(), flops=0, n=0, limit=45056, **more):
    places = [
        pltpu.SMEM if i in smem else pl.ANY if i in free else pltpu.HBM if i in hbm else pltpu.VMEM
        for i in range(n)
    ]
    specs = [pl.BlockSpec(memory_space=place) for place in places]
    return pl.pallas_call(
        body,
        out_shape=tuple(jax.ShapeDtypeStruct(s, t) for s, t in outs),
        in_specs=specs,
        out_specs=tuple(
            pl.BlockSpec(memory_space=pl.ANY if i in free_out else pltpu.VMEM) for i in range(len(outs))
        ),
        scratch_shapes=list(scratch),
        cost_estimate=pl.CostEstimate(flops=flops, bytes_accessed=0, transcendentals=0),
        compiler_params=pltpu.CompilerParams(vmem_limit_bytes=limit << 10),
        **more,
    )


def ring(values, axis, up):
    count = lax.axis_size(axis)
    pairs = [(i, (i + 1) % count) if up else ((i + 1) % count, i) for i in range(count)]
    return lax.ppermute(values, axis, pairs)


def local(
    displacement,
    direction,
    modulus,
    external,
    stiffness,
    master_record,
    pair_face,
    pair_owner,
    pair_row,
    pair_count,
):
    u = displacement.reshape(3 * ZN * YN, XN)
    v = direction.reshape(3 * ZN * YN, XN)
    m = modulus.reshape(ZN * YN, XN)
    request, codes, z_up, z_down = call(
        request_kernel,
        [((OWNERS, 128), I32), ((CHUNKS, 128), I32), ((7, 2, YN, XN), F32), ((7, 1, YN, XN), F32)],
        scratch=[
            pltpu.VMEM((8, 128), I32), pltpu.VMEM((8, 128), I32), pltpu.VMEM((8, 128), I32),
            pltpu.SemaphoreType.DMA((9,)),
        ],
        hbm=tuple(range(6)), n=6, limit=64512,
    )(
        pair_owner.reshape(8, 128), pair_row.reshape(8, 128), pair_face.reshape(8, 128),
        displacement, direction, modulus,
    )
    z_low = ring(z_up, "gz", True).reshape(7 * 2 * YN, XN)
    z_high = ring(z_down, "gz", False).reshape(7 * YN, XN)
    ids = lax.all_to_all(request, GROUPS, split_axis=0, concat_axis=0, tiled=True)

    (table,) = call(table_kernel, [((32, ROWS), F32)], n=2)(master_record, jnp.asarray(table_constants()))
    kin, selector = call(
        slot_kernel, [((CHUNKS, 56, 128), F32), ((OWNERS * CAP, FACES), BF16)],
        scratch=[pltpu.VMEM((56, 256), F32)], smem=(4,), n=5,
    )(u, v, codes, jnp.asarray(slot_constants()), pair_count)
    y_up, y_down = call(side_kernel, [((7 * 2 * 24, XN), F32), ((7 * 24, XN), F32)], n=5)(
        u, v, m, z_low, z_high
    )
    y_low = ring(y_up, "gy", True)
    y_high = ring(y_down, "gy", False)

    (reply,) = call(gather_kernel, [((OWNERS, 8, 128), F32)], n=2, flops=5 << 28)(ids, table)
    x_down, reply = call(
        edge_kernel, [((16, 128), F32), ((OWNERS, 8, 128), F32)], n=8, free=(7,), free_out=(1,),
        input_output_aliases={7: 1},
    )(u, v, m, z_low, z_high, y_low, y_high, reply)
    x_high = ring(x_down, "gx", False)
    replies = lax.all_to_all(reply, GROUPS, split_axis=0, concat_axis=0, tiled=True)

    edges = jnp.stack([lax.axis_index(a).astype(I32) for a in ("gz", "gy", "gx")])
    residual, tangent, last = call(
        element_kernel,
        [((3 * ZN * YN, XN), F32), ((3 * ZN * YN, XN), F32), ((8, 128), F32)],
        scratch=[
            pltpu.VMEM((NODE_ROWS, 128), F32),
            pltpu.VMEM((NODE_ROWS, 128), BF16),
            pltpu.VMEM((NODE_ROWS, 128), BF16),
            pltpu.VMEM((NODE_ROWS, 128), F32),
        ],
        smem=(0,), n=12, flops=1 << 33,
    )(
        edges, u, v, m, external.reshape(3 * ZN * YN, XN), z_low, z_high, y_low, y_high, x_high,
        stiffness, jnp.asarray(element_constants()),
    )
    left = ring(last, "gx", True)
    residual, tangent = call(
        contact_kernel, [((3 * ZN * YN, XN), F32), ((3 * ZN * YN, XN), F32)], n=9, flops=1 << 20
    )(replies, kin, selector, jnp.asarray(contact_constants()), left, u, v, residual, tangent)
    return residual.reshape(3, ZN, YN, XN), tangent.reshape(3, ZN, YN, XN)


def solution(mesh):
    placed = (
        P(None, "gz", "gy", "gx"),
        P(None, "gz", "gy", "gx"),
        P("gz", "gy", "gx"),
        P(None, "gz", "gy", "gx"),
        P(),
        P(None, ("gx", "gy", "gz")),
        P(("gx", "gy", "gz")),
        P(("gx", "gy", "gz"), None),
        P(("gx", "gy", "gz")),
        P(("gx", "gy", "gz")),
    )
    return jax.shard_map(
        local,
        mesh=mesh,
        in_specs=placed,
        out_specs=(P(None, "gz", "gy", "gx"), P(None, "gz", "gy", "gx")),
        check_vma=False,
    )
```

```python
import jax
import jax.numpy as jnp
import numpy as np
from jax import lax
from jax.experimental import pallas as pl
from jax.experimental.pallas import tpu as pltpu
from jax.sharding import PartitionSpec as P

F32 = jnp.float32
BF16 = jnp.bfloat16
I32 = jnp.int32

ZN, YN, XN = 16, 8, 128
ZE, YE = ZN + 3, YN + 3
OWNERS, CAP, PAIRS, ROWS = 64, 32, 1024, 2048
CHUNKS = OWNERS * CAP // 128
FACE_ROWS, FACE_COLS, FACE_LANES = 3, 63, 64
FACES = FACE_ROWS * FACE_LANES
SLABS = 28
TILE = 16
YPITCH = TILE
ZPITCH = YE * TILE
NODE_ROWS = ZE * ZPITCH
Y_UP, Y_DOWN = 272, 144
BLOCK = 9 * TILE
GROUPS = ("gx", "gy")
GROUP = 14


def shapes_1d():
    points = np.array([-np.sqrt(0.6), 0.0, np.sqrt(0.6)])
    gauss = np.array([5.0, 8.0, 5.0]) / 9.0
    line = np.stack(
        [points * (points - 1.0) / 2.0, 1.0 - points * points, points * (points + 1.0) / 2.0],
        axis=1,
    )
    return line, gauss


def halves(values):
    high = np.asarray(values, np.float32).astype(jnp.bfloat16)
    low = (np.asarray(values, np.float64) - high.astype(np.float64)).astype(jnp.bfloat16)
    return high, low


def record_map():
    line, _ = shapes_1d()
    out = np.zeros((32, 27))
    for k in range(3):
        for qy in range(3):
            for qx in range(3):
                q = 3 * qy + qx
                row = k * 8 + q if q < 8 else 24 + k
                for b in range(3):
                    for a in range(3):
                        out[row, 9 * k + 3 * b + a] = line[qy, b] * line[qx, a]
    return halves(out)


def quad_row(part, q):
    return part * 8 + q if q < 8 else 48 + part


def face_x_map():
    line, _ = shapes_1d()
    out = np.zeros((128, 6 * 128))
    for qx in range(3):
        for side in range(2):
            for fx in range(FACE_COLS):
                for a in range(3):
                    out[2 * fx + a, (2 * qx + side) * 128 + side * 64 + fx] = line[qx, a]
    return halves(out)


def face_y_map():
    line, _ = shapes_1d()
    first = np.zeros((56, 6 * 48))
    second = np.zeros((56, 6 * 48))
    for part in range(6):
        for qy in range(3):
            for qx in range(3):
                row = quad_row(part, 3 * qy + qx)
                for b in range(3):
                    first[row, (2 * qx) * 48 + part * 8 + b] = line[qy, b]
                    first[row, (2 * qx + 1) * 48 + part * 8 + 2 + b] = line[qy, b]
                    second[row, (2 * qx) * 48 + part * 8 + 4 + b] = line[qy, b]
    return halves(first), halves(second)


def node_x_map():
    line, _ = shapes_1d()
    out = np.zeros((FACE_LANES, 3 * 128))
    for qx in range(3):
        for fx in range(FACE_COLS):
            for a in range(3):
                out[fx, qx * 128 + 2 * fx + a] = line[qx, a]
    return halves(out)


def node_y_map():
    line, gauss = shapes_1d()
    out = np.zeros((48, 3 * FACE_ROWS * 64))
    for part in range(6):
        for qx in range(3):
            for qy in range(3):
                weight = 0.25 * gauss[qx] * gauss[qy] * (-1.0 if part < 3 else 1.0)
                for fy in range(FACE_ROWS):
                    for b in range(3):
                        column = qx * FACE_ROWS * 64 + fy * 64 + quad_row(part, 3 * qy + qx)
                        out[part * 8 + 2 * fy + b, column] = weight * line[qy, b]
    return halves(out)


def stiffness_places():
    place = np.zeros((BLOCK, 81))
    for block in range(9):
        for p in range(3):
            for c in range(3):
                place[block * TILE + 3 * p + c, block * 9 + 3 * p + c] = 1.0
    fixed = np.zeros((BLOCK, BLOCK))
    for block in range(9):
        fixed[block * TILE + 9, block * TILE + 12] = 1.0
        for p in range(3):
            fixed[10, block * TILE + 9 + p] = 1.0 / 27.0
    fixed[[b * TILE + 9 for b in range(1, 9)], :] = 0.0
    for block in range(1, 9):
        fixed[block * TILE + 9, block * TILE + 12] = 1.0
    return place.astype(np.float32), halves(fixed)


def packed(pieces, rows, columns):
    out = np.zeros((rows, columns), jnp.bfloat16)
    for row, column, piece in pieces:
        out[row : row + piece.shape[0], column : column + piece.shape[1]] = piece
    return out


def element_constants():
    place, fixed = stiffness_places()
    return packed([(0, 0, fixed[0]), (0, 256, fixed[1]), (0, 512, place.astype(jnp.bfloat16))], 144, 640)


def slot_constants():
    along = face_x_map()
    first, second = face_y_map()
    pieces = [
        (0, 0, along[0]), (128, 0, along[1]),
        (256, 0, first[0]), (256, 384, second[0]), (320, 0, first[1]), (320, 384, second[1]),
    ]
    return packed(pieces, 384, 768)


def table_constants():
    high, low = record_map()
    return packed([(0, 0, high), (0, 128, low)], 32, 256)


def contact_constants():
    along, across = node_x_map(), node_y_map()
    pieces = [(0, 0, along[0]), (64, 0, along[1]), (128, 0, across[0]), (176, 0, across[1])]
    return packed(pieces, 224, 576)


def split(values):
    high = values.astype(BF16)
    return high, (values - high.astype(F32)).astype(BF16)


def mm(a, b):
    return jnp.dot(a, b, preferred_element_type=F32)


def mm_nt(a, b):
    return lax.dot_general(a, b, (((1,), (1,)), ((), ())), preferred_element_type=F32)


def mm3(a, b):
    return mm(a[0], b[0]) + (mm(a[0], b[1]) + mm(a[1], b[0]))


def lane_ids(rows):
    return lax.broadcasted_iota(I32, (rows, 128), 1)


def pick_lanes(values, index):
    return jnp.take_along_axis(values, index, axis=1, mode="promise_in_bounds")


def compact(values):
    return (
        values[0:16]
        + pltpu.roll(values[16:32], 32, 1)
        + pltpu.roll(values[32:48], 64, 1)
        + pltpu.roll(values[48:64], 96, 1)
    )


def by_group(lane, parts):
    odd = (lane & 32) != 0
    return jnp.where(lane < 64, jnp.where(odd, parts[1], parts[0]), jnp.where(odd, parts[3], parts[2]))


def swap_groups(quads):
    lane = lane_ids(8)
    moved = [[by_group(lane, [q[(g + r) % 4] for g in range(4)]) for q in quads] for r in range(4)]
    for r in range(1, 4):
        moved[r] = [pltpu.roll(x, 32 * r, 1) for x in moved[r]]
    return [
        [by_group(lane, [moved[(f - g) % 4][i] for f in range(4)]) for g in range(4)]
        for i in range(len(quads))
    ]


def request_kernel(
    owners, rows, sides_in, u, v, m, request, codes, z_up, z_down, owner, row, face, arrived
):
    first = [
        pltpu.make_async_copy(source, to, arrived.at[6 + i])
        for i, (source, to) in enumerate(((owners, owner), (rows, row), (sides_in, face)))
    ]
    for copy in first:
        copy.start()
    layers = []
    for i, (to, start, size) in enumerate(((z_up, ZN - 2, 2), (z_down, 0, 1))):
        part = pl.ds(start, size)
        layers += [
            pltpu.make_async_copy(u.at[:, part], to.at[pl.ds(0, 3)], arrived.at[3 * i]),
            pltpu.make_async_copy(v.at[:, part], to.at[pl.ds(3, 3)], arrived.at[3 * i + 1]),
            pltpu.make_async_copy(m.at[part], to.at[6], arrived.at[3 * i + 2]),
        ]
    for copy in layers:
        copy.start()
    for copy in first:
        copy.wait()
    who = lax.broadcasted_iota(I32, (OWNERS, 128), 0)
    lane = lane_ids(1)
    hits = []
    for t in range(PAIRS // 128):
        hits.append(jnp.where(who == owner[pl.ds(t, 1), :], 1.0, 0.0).astype(F32))
    before = jnp.where(
        lax.broadcasted_iota(I32, (128, 128), 0) < lax.broadcasted_iota(I32, (128, 128), 1), 1.0, 0.0
    ).astype(BF16)
    ranks = mm(jnp.concatenate([h.astype(BF16) for h in hits], axis=0), before)
    base = jnp.zeros((OWNERS, 1), F32)
    places = lax.broadcasted_iota(I32, (128, 128), 0)
    highs, lows, sides, marks = [], [], [], []
    for t in range(PAIRS // 128):
        rank = jnp.sum(hits[t] * (ranks[t * OWNERS : (t + 1) * OWNERS] + base), axis=0, keepdims=True)
        base = base + jnp.sum(hits[t], axis=1, keepdims=True)
        here = places == rank.astype(I32)
        number = row[pl.ds(t, 1), :] + 1
        f = face[pl.ds(t, 1), :]
        f = f + jnp.where(f >= FACE_COLS, 1, 0) + jnp.where(f >= 2 * FACE_COLS, 1, 0) + 1
        spot = lane + t * 128
        numbers = (
            lax.shift_right_logical(number, 6) + 64 * (t // 2),
            (number & 63) + 64 * (lax.shift_right_logical(spot, 6) & 3),
            f,
            spot & 63,
        )
        for to, value in zip((highs, lows, sides, marks), numbers):
            to.append(jnp.where(here, value.astype(F32), 0.0).astype(BF16))
    hit = jnp.concatenate([h.astype(BF16) for h in hits], axis=1)
    high, low, side, mark = (
        mm_nt(hit, jnp.concatenate(to, axis=1)).astype(I32) for to in (highs, lows, sides, marks)
    )
    request[...] = (high & 63) * 64 + (low & 63)
    spots = lax.shift_right_logical(high, 6) * 256 + lax.shift_right_logical(low, 6) * 64 + mark
    codes[...] = compact(spots * 256 + side)
    for copy in layers:
        copy.wait()


def side_kernel(u, v, m, z_low, z_high, y_up, y_down):
    for first, field, comps in ((0, u, 3), (3, v, 3), (6, m, 1)):
        for c in range(comps):
            n = first + c
            for out, h, y in ((y_up, 0, YN - 2), (y_up, 1, YN - 1), (y_down, 0, 0)):
                at = (n * (2 if out is y_up else 1) + h) * ZE
                out[pl.ds(at, ZN), :] = field[pl.ds(c * ZN * YN + y, ZN, stride=YN), :]
                out[pl.ds(at + 16, 8), :] = jnp.zeros((8, 128), F32)
                out[pl.ds(at + 16, 1), :] = z_low[pl.ds((n * 2) * YN + y, 1), :]
                out[pl.ds(at + 17, 1), :] = z_low[pl.ds((n * 2 + 1) * YN + y, 1), :]
                out[pl.ds(at + 18, 1), :] = z_high[pl.ds(n * YN + y, 1), :]


def table_kernel(master, fixed, table, ninth):
    full = mm3((fixed[:, 0:27], fixed[:, 128:155]), split(master[...]))
    table[...] = full[0:24]
    ninth[...] = jnp.concatenate([full[24:28, 0 : ROWS // 2], full[24:28, ROWS // 2 :]], axis=0)


def stiffness_pair(stiffness, fixed):
    places = fixed[:, 512:593]
    high, low = split(stiffness[...])
    lower = (stiffness[...] - high.astype(F32) - low.astype(F32)).astype(BF16)
    spread = [mm_nt(mm(places, part).astype(BF16), places) for part in (high, low, lower)]
    high, low = split((spread[0] + spread[1]) + spread[2])
    return high + fixed[:, 0:144], low + fixed[:, 256:400]


def gather_kernel(ids, table, ninth, reply):
    numbers = jnp.maximum(compact(ids[...]) - 1, 0)
    found = []
    for c in range(CHUNKS):
        number = jnp.broadcast_to(numbers[c : c + 1], (8, 128))
        inside = number & 127
        outside = lax.shift_right_logical(number, 7)
        parts = []
        for f in range(3):
            total = pick_lanes(table[pl.ds(f * 8, 8), 0:128], inside)
            for k in range(1, ROWS // 128):
                piece = pick_lanes(table[pl.ds(f * 8, 8), k * 128 : (k + 1) * 128], inside)
                total = jnp.where(outside == k, piece, total)
            parts.append(total)
        total = pick_lanes(ninth[:, 0:128], inside)
        for k in range(1, ROWS // 256):
            piece = pick_lanes(ninth[:, k * 128 : (k + 1) * 128], inside)
            total = jnp.where((outside & 7) == k, piece, total)
        parts.append(jnp.where(outside < 8, total, pltpu.roll(total, 4, 0)))
        found.append(parts)
    for c, tiles in enumerate(swap_groups(found)):
        for g in range(4):
            reply[g * CHUNKS + c] = tiles[g]


def slab(fields, halos, n, s):
    z_low, z_high, y_low, y_high = halos
    if s < 16:
        return fields[n // 3][pl.ds((n % 3 * ZN + s) * YN, YN), :]
    if s < 18:
        return z_low[pl.ds((n * 2 + s - 16) * YN, YN), :]
    if s < 19:
        return z_high[pl.ds(n * YN, YN), :]
    h, zb = divmod(s - 19, 3)
    if h < 2:
        return y_low[pl.ds((n * 2 + h) * ZE + zb * 8, 8), :]
    return y_high[pl.ds(n * ZE + zb * 8, 8), :]


def edge_kernel(u, v, m, z_low, z_high, y_low, y_high, reply_in, x_down, reply_out):
    fields, halos = (u, v, m), (z_low, z_high, y_low, y_high)
    lane = lane_ids(8)
    down = [jnp.zeros((8, 128), F32) for _ in range(2)]
    for c in range(4):
        for s in range(SLABS):
            k, spot = divmod(c * SLABS + s, 64)
            one = slab(fields, halos, 6 if c == 3 else c, s)
            two = one if c == 3 else slab(fields, halos, 3 + c, s)
            one = pltpu.roll(one, spot, 1) if spot else one
            two = pltpu.roll(two, 64 + spot, 1)
            down[k] = jnp.where(lane == spot, one, jnp.where(lane == 64 + spot, two, down[k]))
    for k in range(2):
        x_down[pl.ds(k * 8, 8), :] = down[k]


def element_kernel(
    edges, u, v, m, external, z_low, z_high, y_low, y_high, x_high, stiffness, fixed,
    residual, tangent, last, nodes, tiles_h, tiles_l, total,
):
    fields, halos = (u, v, m), (z_low, z_high, y_low, y_high)
    lane = lane_ids(8)
    low_half = lane < 64
    spot_of = lane & 63
    at_last = spot_of == 63
    even_even = 2 * spot_of
    odd_odd = 2 * spot_of + 1
    next_next = (2 * spot_of + 2) & 127

    def node_values(group):
        ones = [slab(fields, halos, 6 if c == 3 else c, s) for c, s in group]
        twos = [None if c == 3 else slab(fields, halos, 3 + c, s) for c, s in group]
        found = []
        for index in (even_even, odd_odd, next_next):
            first = [pick_lanes(one, index) for one in ones]
            second = [None if two is None else pick_lanes(two, index) for two in twos]
            found.append([a if b is None else jnp.where(low_half, a, b) for a, b in zip(first, second)])
        for i, (c, s) in enumerate(group):
            k, spot = divmod(c * SLABS + s, 64)
            held = x_high[pl.ds(k * 8, 8), :]
            after = held if spot == 63 else pltpu.roll(held, 63 - spot, 1)
            found[2][i] = jnp.where(at_last, after, found[2][i])
        return list(zip(*found))

    def put(value, s, at):
        if s < 19:
            z = s + 2 if s < 16 else (0, 1, 18)[s - 16]
            nodes[pl.ds(z * ZPITCH + 2 * YPITCH + at, 8, stride=YPITCH), :] = value
            return
        h, zb = divmod(s - 19, 3)
        base = (0, 1, 10)[h] * YPITCH + at
        if zb < 2:
            nodes[pl.ds((2 + zb * 8) * ZPITCH + base, 8, stride=ZPITCH), :] = value
        else:
            nodes[pl.ds(base, 1), :] = value[0:1]
            nodes[pl.ds(ZPITCH + base, 1), :] = value[1:2]
            nodes[pl.ds(18 * ZPITCH + base, 1), :] = value[2:3]

    todo = [(c, s) for c in range(4) for s in range(SLABS)]
    for start in range(0, len(todo), GROUP):
        group = todo[start : start + GROUP]
        values = node_values(group)
        for (c, s), three in zip(group, values):
            first, step = (9, 1) if c == 3 else (c, 3)
            for p in range(3):
                put(three[p], s, first + step * p)

    sub = lax.broadcasted_iota(I32, (TILE, 128), 0)
    one = jnp.where(sub == 12, 1.0, 0.0)

    def halve(z, carry):
        places = [pl.ds(pl.multiple_of(z * ZPITCH + y * YPITCH, TILE), TILE) for y in range(YE)]
        pairs = [split(jnp.where(sub < 12, nodes[at, :], one)) for at in places]
        for at, (high, low) in zip(places, pairs):
            tiles_h[at, :] = high
            tiles_l[at, :] = low
        return carry

    lax.fori_loop(0, ZE, halve, 0)

    x_last = jnp.where(edges[2] == lax.axis_size("gx") - 1, 63, 64)
    inside_x = jnp.where((lane_ids(1) & 63) < x_last, 1.0, 0.0)
    y_first = jnp.where(edges[1] == 0, 1, 0)
    y_last = jnp.where(edges[1] == lax.axis_size("gy") - 1, 3, 4)
    z_first = jnp.where(edges[0] == 0, 1, 0)
    z_last = jnp.where(edges[0] == lax.axis_size("gz") - 1, 7, 8)
    left_high, left_low = stiffness_pair(stiffness, fixed)

    total[pl.ds(0, ZPITCH), :] = jnp.zeros((ZPITCH, 128), F32)

    def inside_of(k, j):
        return (k >= z_first) & (k <= z_last) & (j >= y_first) & (j <= y_last)

    def products(elements):
        operands = []
        for tiles in (tiles_h, tiles_l):
            columns = []
            for k, j in elements:
                starts = [pl.multiple_of((2 * k + r) * ZPITCH + 2 * j * YPITCH, TILE) for r in range(3)]
                columns.append(jnp.concatenate([tiles[pl.ds(a, 3 * TILE), :] for a in starts], axis=0))
            operands.append(jnp.concatenate(columns, axis=1))
        both = mm3((left_high, left_low), operands)
        forces = []
        for i, (k, j) in enumerate(elements):
            mine = both[:, i * 128 : (i + 1) * 128]
            forces.append(mine * jnp.where(inside_of(k, j), mine[10:11] * inside_x, 0.0))
        return forces

    def part(force, r, q):
        return force[(3 * r + q) * TILE : (3 * r + q + 1) * TILE]

    def place_of(z, y):
        return pl.ds(pl.multiple_of(z * ZPITCH + y * YPITCH, TILE), TILE)

    def layers(i, carry):
        shared = None
        for j in range(5):
            one, two = products([(2 * i, j), (2 * i + 1, j)])
            for q in range(3):
                sums = [part(one, 0, q), part(one, 1, q), part(one, 2, q) + part(two, 0, q), part(two, 1, q), part(two, 2, q)]
                if q == 0 and shared is not None:
                    sums = [a + b for a, b in zip(sums, shared)]
                if q == 2 and j < 4:
                    shared = sums
                    continue
                y = 2 * j + q
                sums[0] = sums[0] + total[place_of(4 * i, y), :]
                for r in range(5):
                    total[place_of(4 * i + r, y), :] = sums[r]
        return carry

    lax.fori_loop(0, 4, layers, 0)
    last_layer = products([(8, 0), (8, 1)]) + products([(8, 2), (8, 3)]) + products([(8, 4)])
    for r in range(3):
        for y in range(YE):
            held = [part(last_layer[j], r, y - 2 * j) for j in range(5) if 0 <= y - 2 * j <= 2]
            held = held + [total[place_of(16, y), :]] if r == 0 else held
            total[place_of(16 + r, y), :] = sum(held[1:], held[0])

    half = lax.shift_right_logical(lane, 1)
    weave_u = half + jnp.where((lane & 1) == 0, 0, 64)
    weave_v = half + jnp.where((lane & 1) == 0, 64, 0)
    at_first = spot_of == 0
    sent = jnp.zeros((8, 128), F32)
    for start in range(0, ZN, 4):
        layer = range(start, start + 4)

        def rows(z, row):
            return total[pl.ds((z + 2) * ZPITCH + 2 * YPITCH + row, 8, stride=YPITCH), :]

        held = [rows(z, 9) for z in layer]
        p0 = [rows(z, c) for z in layer for c in range(3)]
        p1 = [rows(z, 3 + c) for z in layer for c in range(3)]
        p2 = [rows(z, 6 + c) for z in layer for c in range(3)]
        after = [pltpu.roll(x, 1, 1) for x in held + p2]
        odd = [pltpu.roll(x, 64, 1) for x in p1]
        for i, z in enumerate(layer):
            sent = jnp.where(spot_of == 48 + z, pltpu.roll(held[i], (z - 15) % 128, 1), sent)
            for c in range(3):
                moved = pltpu.roll(p2[3 * i + c], (c * 16 + z - 63) % 128, 1)
                sent = jnp.where(spot_of == c * 16 + z, moved, sent)
        after = [jnp.where(at_first, 0.0, x) for x in after]
        even = [a + b for a, b in zip(p0, after[4:])]
        mass = [pick_lanes(jnp.where(low_half, a + b, a), weave_u) for a, b in zip(held, after)]
        inner = [pick_lanes(jnp.where(low_half, a, b), weave_u) for a, b in zip(even, odd)]
        image = [pick_lanes(jnp.where(low_half, b, a), weave_v) for a, b in zip(even, odd)]
        results = []
        for i, z in enumerate(layer):
            for c in range(3):
                where = pl.ds((c * ZN + z) * YN, YN)
                uu, vv = u[where, :], v[where, :]
                square = uu * uu * mass[i]
                results.append(
                    (
                        where,
                        inner[3 * i + c] + 0.1 * square * uu - external[where, :],
                        image[3 * i + c] + 0.3 * square * vv,
                    )
                )
        for where, res, tan in results:
            residual[where, :] = res
            tangent[where, :] = tan
    last[...] = sent


def slot_kernel(u, v, codes, fixed, count, kin, selector, quads):
    plane = jnp.concatenate(
        [field[pl.ds(c * ZN * YN, YN), :] for field in (u, v) for c in range(3)], axis=0
    )
    wide = mm3(split(plane), (fixed[0:128, :], fixed[128:256, :]))
    tall = split(jnp.concatenate([wide[:, i * 128 : (i + 1) * 128] for i in range(6)], axis=0))
    for first, to in ((0, 0), (384, 128)):
        pair = fixed[256:312, first : first + 288], fixed[320:376, first : first + 288]
        quads[:, to : to + 128] = mm3(pair, tall)
    spots = lax.shift_right_logical(codes[...], 8)
    slot_faces = jnp.where(spots < count[0], codes[...] & 255, 0)
    columns = jnp.concatenate([slot_faces.astype(F32), jnp.zeros((112, 128), F32)], axis=0).T
    face_ids = (lax.broadcasted_iota(I32, (128, FACES), 1) + 1).astype(F32)
    for c in range(CHUNKS):
        slot_face = slot_faces[c : c + 1]
        index = jnp.maximum(jnp.broadcast_to(slot_face, (8, 128)) - 1, 0)
        inside, outside = index & 127, index >= 128
        for i in range(7):
            kin[c, pl.ds(i * 8, 8), :] = jnp.where(
                outside,
                pick_lanes(quads[pl.ds(i * 8, 8), 128:256], inside),
                pick_lanes(quads[pl.ds(i * 8, 8), 0:128], inside),
            )
        selector[pl.ds(c * 128, 128), :] = jnp.where(face_ids == columns[:, c : c + 1], 1.0, 0.0).astype(BF16)


def contact_kernel(replies, kin, selector, fixed, left, u, v, res_in, tan_in, residual, tangent):
    values_h, values_l = [], []
    records = swap_groups([[replies[g * CHUNKS + c] for g in range(4)] for c in range(CHUNKS)])
    for c in range(CHUNKS):
        m = records[c]

        def point(m0, m1, m2, k):
            gap = m0 + m1 * k[0] + m2 * k[1] + k[2]
            scaled = -2.0 * gap
            small = jnp.exp(-jnp.abs(scaled))
            pressure = 2.0 * (jnp.maximum(scaled, 0.0) + jnp.log1p(small))
            slope = 4.0 * jnp.where(scaled >= 0.0, 1.0, small) / (1.0 + small)
            push = slope * (m1 * k[3] + m2 * k[4] + k[5])
            return pressure * m1, pressure * m2, pressure, push * m1, push * m2, push

        main = point(m[0], m[1], m[2], [kin[c, pl.ds(i * 8, 8), :] for i in range(6)])
        ends = kin[c, pl.ds(48, 8), :]
        ninth = point(m[3][0:1], m[3][1:2], m[3][2:3], [ends[i : i + 1] for i in range(6)])
        stack = jnp.concatenate(list(main) + list(ninth) + [jnp.zeros((10, 128), F32)], axis=0)
        high, low = split(stack)
        values_h.append(high)
        values_l.append(low)
    values = jnp.concatenate(
        [jnp.concatenate(values_h, axis=1), jnp.concatenate(values_l, axis=1)], axis=0
    )
    sums = mm(values, selector[...])
    sums = sums[0:64] + sums[64:128]
    sums = jnp.concatenate([sums[:, 0:64], sums[:, 64:128], sums[:, 128:192]], axis=0)
    along = mm3(split(sums), (fixed[0:64, 0:384], fixed[64:128, 0:384]))
    tall = split(jnp.concatenate([along[:, i * 128 : (i + 1) * 128] for i in range(3)], axis=0))
    plane = mm3((fixed[128:176, :], fixed[176:224, :]), tall)
    at_first = lane_ids(8) == 0
    came = left[...]
    for z in range(ZN):
        mass = pltpu.roll(came, 80 - z, 1)
        for c in range(3):
            where = pl.ds((c * ZN + z) * YN, YN)
            uu, vv = u[where, :], v[where, :]
            square = uu * uu * mass
            spot = c * 16 + z
            inner = came if spot == 0 else pltpu.roll(came, 128 - spot, 1)
            image = pltpu.roll(came, 64 - spot, 1)
            res = res_in[where, :] + jnp.where(at_first, inner + 0.1 * square * uu, 0.0)
            tan = tan_in[where, :] + jnp.where(at_first, image + 0.3 * square * vv, 0.0)
            if z == 0:
                res = res + plane[c * 8 : c * 8 + 8]
                tan = tan + plane[24 + c * 8 : 32 + c * 8]
            residual[where, :] = res
            tangent[where, :] = tan


def call(body, outs, scratch=(), smem=(), free=(), hbm=(), free_out=(), flops=0, n=0, limit=45056, **more):
    places = [
        pltpu.SMEM if i in smem else pl.ANY if i in free else pltpu.HBM if i in hbm else pltpu.VMEM
        for i in range(n)
    ]
    specs = [pl.BlockSpec(memory_space=place) for place in places]
    return pl.pallas_call(
        body,
        out_shape=tuple(jax.ShapeDtypeStruct(s, t) for s, t in outs),
        in_specs=specs,
        out_specs=tuple(
            pl.BlockSpec(memory_space=pl.ANY if i in free_out else pltpu.VMEM) for i in range(len(outs))
        ),
        scratch_shapes=list(scratch),
        cost_estimate=pl.CostEstimate(flops=flops, bytes_accessed=0, transcendentals=0),
        compiler_params=pltpu.CompilerParams(vmem_limit_bytes=limit << 10),
        **more,
    )


def ring(values, axis, up):
    count = lax.axis_size(axis)
    pairs = [(i, (i + 1) % count) if up else ((i + 1) % count, i) for i in range(count)]
    return lax.ppermute(values, axis, pairs)


def local(
    displacement,
    direction,
    modulus,
    external,
    stiffness,
    master_record,
    pair_face,
    pair_owner,
    pair_row,
    pair_count,
):
    u = displacement.reshape(3 * ZN * YN, XN)
    v = direction.reshape(3 * ZN * YN, XN)
    m = modulus.reshape(ZN * YN, XN)
    request, codes, z_up, z_down = call(
        request_kernel,
        [((OWNERS, 128), I32), ((CHUNKS, 128), I32), ((7, 2, YN, XN), F32), ((7, 1, YN, XN), F32)],
        scratch=[
            pltpu.VMEM((8, 128), I32), pltpu.VMEM((8, 128), I32), pltpu.VMEM((8, 128), I32),
            pltpu.SemaphoreType.DMA((9,)),
        ],
        hbm=tuple(range(6)), n=6, limit=64512,
    )(
        pair_owner.reshape(8, 128), pair_row.reshape(8, 128), pair_face.reshape(8, 128),
        displacement, direction, modulus,
    )
    z_low = ring(z_up, "gz", True).reshape(7 * 2 * YN, XN)
    z_high = ring(z_down, "gz", False).reshape(7 * YN, XN)
    ids = lax.all_to_all(request, GROUPS, split_axis=0, concat_axis=0, tiled=True)

    table, ninth = call(table_kernel, [((24, ROWS), F32), ((8, ROWS // 2), F32)], n=2)(
        master_record, jnp.asarray(table_constants())
    )
    kin, selector = call(
        slot_kernel, [((CHUNKS, 56, 128), F32), ((OWNERS * CAP, FACES), BF16)],
        scratch=[pltpu.VMEM((56, 256), F32)], smem=(4,), n=5,
    )(u, v, codes, jnp.asarray(slot_constants()), pair_count)
    y_up, y_down = call(side_kernel, [((Y_UP, XN), F32), ((Y_DOWN, XN), F32)], n=5)(
        u, v, m, z_low, z_high
    )
    y_low = ring(y_up, "gy", True)
    y_high = ring(y_down, "gy", False)

    (reply,) = call(gather_kernel, [((OWNERS, 8, 128), F32)], n=3, flops=1 << 30)(ids, table, ninth)
    x_down, reply = call(
        edge_kernel, [((16, 128), F32), ((OWNERS, 8, 128), F32)], n=8, free=(7,), free_out=(1,),
        input_output_aliases={7: 1},
    )(u, v, m, z_low, z_high, y_low, y_high, reply)
    x_high = ring(x_down, "gx", False)
    replies = lax.all_to_all(reply, GROUPS, split_axis=0, concat_axis=0, tiled=True)

    edges = jnp.stack([lax.axis_index(a).astype(I32) for a in ("gz", "gy", "gx")])
    residual, tangent, last = call(
        element_kernel,
        [((3 * ZN * YN, XN), F32), ((3 * ZN * YN, XN), F32), ((8, 128), F32)],
        scratch=[
            pltpu.VMEM((NODE_ROWS, 128), F32),
            pltpu.VMEM((NODE_ROWS, 128), BF16),
            pltpu.VMEM((NODE_ROWS, 128), BF16),
            pltpu.VMEM((NODE_ROWS, 128), F32),
        ],
        smem=(0,), n=12, flops=1 << 33,
    )(
        edges, u, v, m, external.reshape(3 * ZN * YN, XN), z_low, z_high, y_low, y_high, x_high,
        stiffness, jnp.asarray(element_constants()),
    )
    left = ring(last, "gx", True)
    residual, tangent = call(
        contact_kernel, [((3 * ZN * YN, XN), F32), ((3 * ZN * YN, XN), F32)], n=9, flops=1 << 20
    )(replies, kin, selector, jnp.asarray(contact_constants()), left, u, v, residual, tangent)
    return residual.reshape(3, ZN, YN, XN), tangent.reshape(3, ZN, YN, XN)


def solution(mesh):
    placed = (
        P(None, "gz", "gy", "gx"),
        P(None, "gz", "gy", "gx"),
        P("gz", "gy", "gx"),
        P(None, "gz", "gy", "gx"),
        P(),
        P(None, ("gx", "gy", "gz")),
        P(("gx", "gy", "gz")),
        P(("gx", "gy", "gz"), None),
        P(("gx", "gy", "gz")),
        P(("gx", "gy", "gz")),
    )
    return jax.shard_map(
        local,
        mesh=mesh,
        in_specs=placed,
        out_specs=(P(None, "gz", "gy", "gx"), P(None, "gz", "gy", "gx")),
        check_vma=False,
    )
```
